256 devices in a mesh: chan: 16 (over y, x), win: 16 (over z, core).
Axes of the slice: x: 4, y: 4, z: 8, core: 2. Of those that a mesh axis runs over, the one named last changes fastest.
Arguments:
- spectra: float32 [2, 1024, 32, 2048], P(None, 'win', None, 'chan'), may hold values from -180 to 180
- quality_mask: int32 [1024, 2048], P('win', 'chan'), may hold values 0 or 1
Outputs:
- stacked: float32 [32, 2, 2048, 2048], P('win', None, 'chan')
The draws below stay inside these ranges and needn't reach their ends.
All inputs are finite; a program needn't handle non-finite values. No bound on the sum of `quality_mask` on one device may be relied on, other than what follows from the above.
Results may differ from the reference program's by a relative error of at most 0.0028.
Values may be sent and summed in bfloat16 or wider, within the bound.
A program may use at most 64 MiB of HBM per device.

```python
import math
import jax
import jax.numpy as jnp
from jax import lax

CHANNELS = 2048
FREQ = 32
WINDOWS = 1024


def draw_spectra(key, part):
    key = jax.random.fold_in(key, 11)
    key_base, key_bins, key_rows = jax.random.split(key, 3)
    shape = (2, WINDOWS, FREQ, CHANNELS)
    bin_scale = jnp.exp(jax.random.uniform(key_bins, (1, 1, FREQ, CHANNELS), jnp.float32, 0.0, math.log(10.0)))
    row_scale = jnp.exp(jax.random.uniform(key_rows, (1, WINDOWS, 1, CHANNELS), jnp.float32, math.log(0.3), math.log(3.0)))
    base = jnp.clip(jax.random.normal(key_base, shape, jnp.float32), -6.0, 6.0)
    return base * bin_scale * row_scale


def with_ends(result, key, low, top_value):
    longest = result.shape.index(max(result.shape))
    spots = []
    for shift in (0, 1):
        where = [jax.random.randint(jax.random.fold_in(key, axis), (), 0, length) for axis, length in enumerate(result.shape)]
        where[longest] = (where[longest] + shift) % result.shape[longest]
        spots.append(tuple(where))
    return result.at[spots[0]].set(low).at[spots[1]].set(top_value)


def setup_inputs(seed: int = 0) -> dict:
    splits = jax.random.split(jax.random.key(seed), 3)
    spectra = draw_spectra(jax.random.fold_in(splits[2], 71), 0)
    quality_mask = with_ends((jax.random.randint(splits[1], (WINDOWS, CHANNELS), 0, 8) < 7).astype(jnp.int32), jax.random.fold_in(splits[1], 1), 0, 1)
    return {"spectra": spectra, "quality_mask": quality_mask}


def reference(spectra, quality_mask):
    rms_level = jnp.sqrt(lax.optimization_barrier(jnp.mean(spectra * spectra, axis=(0, 2))) + 1e-06)
    factor = quality_mask.astype(jnp.float32) / rms_level
    whitened = (spectra * factor[None, :, None, :]).astype(jnp.bfloat16)
    rotated = jnp.stack([whitened[1], -whitened[0]])
    by_bin = jnp.transpose(jnp.stack([whitened, rotated]), (3, 0, 1, 2, 4))
    inv_root = 1.0 / math.sqrt(WINDOWS)

    def one_bin(pair_bin):
        flat_own = pair_bin[0].reshape(2 * WINDOWS, CHANNELS)
        flat_rot = pair_bin[1].reshape(2 * WINDOWS, CHANNELS)
        real_part = jnp.dot(flat_own.T, flat_own, preferred_element_type=jnp.float32)
        imag_part = jnp.dot(flat_rot.T, flat_own, preferred_element_type=jnp.float32)
        return jnp.stack([real_part, imag_part]) * inv_root
    return lax.map(one_bin, by_bin)
```

```python
import functools

import jax
import jax.numpy as jnp
from jax import lax
from jax.experimental import pallas as pl
from jax.experimental.pallas import tpu as pltpu
from jax.sharding import PartitionSpec as P

MESH = pl.DeviceIdType.MESH
F32, BF16 = jnp.float32, jnp.bfloat16

WIN = 16
SIDE = 4
BINS = 2
CH = 128
LW = 64
HALF = LW // 2
DEEP = WIN * HALF
FREQ = WIN * BINS


def mod4(v):
    return lax.rem(v + 2 * SIDE, SIDE)


def kernel(
    spec, mask, out,
    spec_v, send_v, g, t_own, t_row, acc, cross, res_send, res_recv, stage,
    in_sem, a_send, a_recv, g_send, g_recv, r_send, r_recv, s_send, s_recv, o_sem,
):
    chan, win = lax.axis_index("chan"), lax.axis_index("win")
    x, y = lax.rem(chan, SIDE), lax.div(chan, SIDE)

    def at(dx, dy):
        return mod4(y + dy) * SIDE + mod4(x + dx)

    barrier = pltpu.get_barrier_semaphore()

    def greet(k, _):
        pl.semaphore_signal(
            barrier, inc=1, device_id=(chan, lax.rem(win + k, WIN)), device_id_type=MESH
        )
        return 0

    lax.fori_loop(1, WIN, greet, 0)
    for d in (1, 2, 3):
        pl.semaphore_signal(barrier, inc=1, device_id=(at(d, 0), win), device_id_type=MESH)
        pl.semaphore_signal(barrier, inc=1, device_id=(at(0, d), win), device_id_type=MESH)

    rows = HALF * FREQ
    loads = [
        pltpu.make_async_copy(
            spec.at[:, pl.ds(h * rows, rows), :], spec_v.at[:, pl.ds(h * rows, rows), :], in_sem.at[h]
        )
        for h in range(2)
    ]
    for load in loads:
        load.start()

    def whiten(h):
        base = h * rows

        def add(f, total):
            for p in range(2):
                v = spec_v[p, pl.ds(base + f, HALF, stride=FREQ), :]
                total = total + v * v
            return total

        total = lax.fori_loop(0, FREQ, add, jnp.zeros((HALF, CH), F32))
        rms = jnp.sqrt(total * (1.0 / (2 * FREQ)) + 1e-6)
        factor = mask[pl.ds(h * HALF, HALF), :].astype(F32) / rms

        def scale(dst, _):
            for b in range(BINS):
                for p in range(2):
                    v = spec_v[p, pl.ds(base + dst * BINS + b, HALF, stride=FREQ), :]
                    send_v[h, b, dst, p] = (v * factor).astype(BF16)
            return 0

        lax.fori_loop(0, WIN, scale, 0)

    mine = pl.ds(pl.multiple_of(win * HALF, HALF), HALF)

    def spread(b, h):
        def one(k, _):
            dst = lax.rem(win + k, WIN)
            pltpu.make_async_remote_copy(
                src_ref=send_v.at[h, b, dst],
                dst_ref=g.at[0, b, h, :, mine, :],
                send_sem=a_send.at[b, h],
                recv_sem=a_recv.at[b, h],
                device_id=(chan, dst),
                device_id_type=MESH,
            ).start()
            return 0

        lax.fori_loop(1, WIN, one, 0)
        g[0, b, h, :, mine, :] = send_v[h, b, win]

    def spread_all(b, h):
        others = g.at[0, b, h, :, pl.ds(0, DEEP - HALF), :]
        return pltpu.make_async_remote_copy(
            src_ref=others, dst_ref=others, send_sem=a_send.at[b, h], recv_sem=a_recv.at[b, h],
            device_id=(chan, win), device_id_type=MESH,
        )

    sides = ((1, 0, 3), (-1, 0, 1), (0, 1, 6), (0, -1, 4))

    def direct(b, h):
        return [
            pltpu.make_async_remote_copy(
                src_ref=g.at[0, b, h], dst_ref=g.at[slot, b, h],
                send_sem=g_send.at[slot, b, h], recv_sem=g_recv.at[slot, b, h],
                device_id=(at(dx, dy), win), device_id_type=MESH,
            )
            for dx, dy, slot in sides
        ]

    def relay(b, h):
        return [
            pltpu.make_async_remote_copy(
                src_ref=g.at[slot, b, h, p], dst_ref=g.at[2 + 3 * (slot // 4), b, h, p],
                send_sem=r_send.at[slot, b, h], recv_sem=r_recv.at[slot, b, h],
                device_id=(at(dx, dy), win), device_id_type=MESH,
            )
            for (dx, dy, slot), p in zip(sides, (0, 1, 0, 1))
        ]

    def turned(slot, b, h, dst):
        a0, a1 = g[slot, b, h, 0].T, g[slot, b, h, 1].T
        dst[pl.ds(0, CH), pl.ds(0, DEEP)] = a0
        dst[pl.ds(0, CH), pl.ds(DEEP, DEEP)] = a1
        dst[pl.ds(CH, CH), pl.ds(0, DEEP)] = a1
        dst[pl.ds(CH, CH), pl.ds(DEEP, DEEP)] = -a0

    def product(lhs, slot, b, h):
        return jnp.dot(
            lhs[...], g[slot, b, h].reshape(2 * DEEP, CH), preferred_element_type=F32
        )

    scaling = 1.0 / 32.0

    def own(slot, b, h):
        part = product(t_own.at[b, h], slot, b, h)
        if h == 0:
            acc[slot, b] = part
        else:
            acc[slot, b] = (acc[slot, b] + part) * scaling

    def emit(value_ref, b, dx, dy):
        col = pl.multiple_of(at(dx, dy) * CH, CH)
        for k in range(2):
            pltpu.make_async_copy(
                value_ref.at[pl.ds(k * CH, CH), :], out.at[b, k, :, pl.ds(col, CH)], o_sem
            ).start()

    def give(value, dx, dy, b):
        n = (dx - 1) * 3 + (dy - 1)
        at_row = (3 - dx) * 3 + (dy - 1)
        at_col = (dx - 1) * 3 + (3 - dy)
        res_send[n, 0] = value.astype(BF16)
        res_send[n, 1, pl.ds(0, CH), :] = value[:CH].T.astype(BF16)
        res_send[n, 1, pl.ds(CH, CH), :] = (-value[CH:]).T.astype(BF16)
        for side, slot, dev in ((0, at_row, at(dx, 0)), (1, at_col, at(0, dy))):
            pltpu.make_async_remote_copy(
                src_ref=res_send.at[n, side], dst_ref=res_recv.at[slot, b],
                send_sem=s_send.at[n, side], recv_sem=s_recv.at[slot, b],
                device_id=(dev, win), device_id_type=MESH,
            ).start()

    def pair(lhs, dx, dy, b, h, keep):
        part = product(lhs, 3 + dy, b, h)
        if h == 0:
            cross[keep] = part
        else:
            give((cross[keep] + part) * scaling, dx, dy, b)

    def early(b, h):
        def one(i, _):
            own(i + lax.div(i, 2), b, h)
            return 0

        lax.fori_loop(0, 5, one, 0)

    def late(b, h):
        for slot in (2, 5):
            own(slot, b, h)
        near = 1 if b == 0 else 3
        turned(near, b, h, t_row.at[2, h])
        turned(2, b, h, t_row.at[b, h])

        def one(i, _):
            pair(t_row.at[2, h], near, i + 1, b, h, i)
            return 0

        lax.fori_loop(0, 3, one, 0)
        pair(t_row.at[b, h], 2, near, b, h, 3)
        if h == 1:
            for slot in range(7):
                emit(acc.at[slot, b], b, slot if slot < 4 else 0, slot - 3 if slot > 3 else 0)

    units = [(b, h) for b in range(BINS) for h in range(2)]

    loads[0].wait()
    whiten(0)
    pl.semaphore_wait(barrier, WIN - 1 + 2 * (SIDE - 1))
    spread(0, 0)
    loads[1].wait()
    whiten(1)
    spread(0, 1)
    for step in range(len(units) + 2):
        if step < len(units):
            unit = units[step]
            spread_all(*unit).wait_recv()
            for copy in direct(*unit):
                copy.start()
            if step + 2 < len(units):
                spread(*units[step + 2])
            turned(0, *unit, t_own.at[unit])
        if 0 <= step - 1 < len(units):
            unit = units[step - 1]
            for copy, onward in zip(direct(*unit), relay(*unit)):
                copy.wait_recv()
                onward.start()
            early(*unit)
        if 0 <= step - 2 < len(units):
            unit = units[step - 2]
            for copy in relay(*unit):
                copy.wait_recv()
            late(*unit)

    bin_here = lax.div(x, 2)
    value = product(t_row.at[bin_here, 0], 5, bin_here, 0)
    value = value + product(t_row.at[bin_here, 1], 5, bin_here, 1)
    give(value * scaling, 2, 2, bin_here)

    def arrived(slot, b):
        return pltpu.make_async_remote_copy(
            src_ref=res_recv.at[slot, b], dst_ref=res_recv.at[slot, b],
            send_sem=s_send.at[slot, 0], recv_sem=s_recv.at[slot, b],
            device_id=(chan, win), device_id_type=MESH,
        )

    for b in range(BINS):
        def take(n, _):
            arrived(n, b).wait_recv()
            stage[n, b] = res_recv[n, b].astype(F32)
            emit(stage.at[n, b], b, lax.div(n, 3) + 1, lax.rem(n, 3) + 1)
            return 0

        lax.fori_loop(0, 9, take, 0)

    for unit in units:
        spread_all(*unit).wait_send()
        for copy in direct(*unit) + relay(*unit):
            copy.wait_send()

    def gone(n, _):
        for side in range(2):
            pltpu.make_async_remote_copy(
                src_ref=res_send.at[n, side], dst_ref=res_send.at[n, side],
                send_sem=s_send.at[n, side], recv_sem=s_recv.at[n, 0],
                device_id=(chan, win), device_id_type=MESH,
            ).wait_send()
        return 0

    lax.fori_loop(0, 9, gone, 0)
    pltpu.make_async_copy(out, out, o_sem).wait()


def body(spectra, quality_mask):
    flat = spectra.reshape(2, LW * FREQ, CH)
    dma = pltpu.SemaphoreType.DMA
    return pl.pallas_call(
        kernel,
        out_shape=jax.ShapeDtypeStruct((BINS, 2, CH, CH * SIDE * SIDE), F32),
        in_specs=[pl.BlockSpec(memory_space=pl.ANY), pl.BlockSpec(memory_space=pltpu.VMEM)],
        out_specs=pl.BlockSpec(memory_space=pl.ANY),
        scratch_shapes=[
            pltpu.VMEM((2, LW * FREQ, CH), F32),
            pltpu.VMEM((2, BINS, WIN, 2, HALF, CH), BF16),
            pltpu.VMEM((7, BINS, 2, 2, DEEP, CH), BF16),
            pltpu.VMEM((BINS, 2, 2 * CH, 2 * DEEP), BF16),
            pltpu.VMEM((3, 2, 2 * CH, 2 * DEEP), BF16),
            pltpu.VMEM((7, BINS, 2 * CH, CH), F32),
            pltpu.VMEM((4, 2 * CH, CH), F32),
            pltpu.VMEM((9, 2, 2 * CH, CH), BF16),
            pltpu.VMEM((9, BINS, 2 * CH, CH), BF16),
            pltpu.VMEM((9, BINS, 2 * CH, CH), F32),
            dma((2,)),
            dma((BINS, 2)),
            dma((BINS, 2)),
            dma((7, BINS, 2)),
            dma((7, BINS, 2)),
            dma((7, BINS, 2)),
            dma((7, BINS, 2)),
            dma((9, 2)),
            dma((9, BINS)),
            dma(()),
        ],
        compiler_params=pltpu.CompilerParams(
            collective_id=0, has_side_effects=True, vmem_limit_bytes=48 * 1024 * 1024
        ),
        cost_estimate=pl.CostEstimate(
            flops=6_200_000_000, bytes_accessed=6 * 1024 * 1024, transcendentals=0
        ),
    )(flat, quality_mask)


def solution(mesh):
    placed = (P(None, "win", None, "chan"), P("win", "chan"))
    return jax.shard_map(
        body, mesh=mesh, in_specs=placed, out_specs=P("win", None, "chan", None), check_vma=False
    )
```

```python
import jax
import jax.numpy as jnp
from jax import lax
from jax.experimental import pallas as pl
from jax.experimental.pallas import tpu as pltpu
from jax.sharding import PartitionSpec as P

MESH = pl.DeviceIdType.MESH
F32, BF16 = jnp.float32, jnp.bfloat16

WIN = 16
SIDE = 4
BINS = 2
FREQ = WIN * BINS
CH = 128
LW = 64
PARTS = 2
PW = LW // PARTS
AHEAD = 2
UNITS = BINS * PARTS
DEEP = WIN * PW
ROWS = PW * FREQ
SCALE = 1.0 / 32.0

PLACES = ((0, 0), (1, 0), (2, 0), (1, 1), (0, 1), (0, 2))
FOREIGN = ((-1, 0), (0, -1), (-1, -1), (-1, 1), (1, -1), (-2, 1), (2, -1), (1, -2), (-1, 2), (2, 2))
MATES = ((1, 0), (-1, 0), (2, 0), (0, 1), (0, -1), (0, 2), (1, 1), (-1, -1))


def kernel(
    spec, mask_hbm, out,
    spec_v, mask, send_v, g, turned, acc, res_send, res_recv,
    in_sem, a_send, a_recv, d_send, d_recv, r_send, r_recv, s_send, s_recv,
):
    chan, win = lax.axis_index("chan"), lax.axis_index("win")
    x, y = lax.rem(chan, SIDE), lax.div(chan, SIDE)
    way = 1 - 2 * lax.rem(win, 2)

    def at(place):
        dx, dy = place
        return lax.rem(y + way * dy + 2 * SIDE, SIDE) * SIDE + lax.rem(x + way * dx + 2 * SIDE, SIDE)

    barrier = pltpu.get_barrier_semaphore()

    def greet(k, _):
        pl.semaphore_signal(
            barrier, inc=1, device_id=(chan, lax.rem(win + k, WIN)), device_id_type=MESH
        )
        return 0

    lax.fori_loop(1, WIN, greet, 0)
    for place in MATES:
        pl.semaphore_signal(barrier, inc=1, device_id=(at(place), win), device_id_type=MESH)

    loads = [pltpu.make_async_copy(mask_hbm, mask, in_sem.at[PARTS])]
    for q in range(PARTS):
        rows = pl.ds(q * ROWS, ROWS)
        loads.append(pltpu.make_async_copy(spec.at[:, rows, :], spec_v.at[:, rows, :], in_sem.at[q]))
    for load in loads:
        load.start()

    def whiten(q):
        def add(f, total):
            for p in range(2):
                v = spec_v[p, pl.ds(q * ROWS + f, PW, stride=FREQ), :]
                total = total + v * v
            return total

        total = lax.fori_loop(0, FREQ, add, jnp.zeros((PW, CH), F32))
        rms = jnp.sqrt(total * (1.0 / (2 * FREQ)) + 1e-6)
        factor = mask[pl.ds(q * PW, PW), :].astype(F32) / rms

        def scale(dst, _):
            for b in range(BINS):
                for p in range(2):
                    v = spec_v[p, pl.ds(q * ROWS + dst * BINS + b, PW, stride=FREQ), :]
                    send_v[b * PARTS + q, dst, p] = (v * factor).astype(BF16)
            return 0

        lax.fori_loop(0, WIN, scale, 0)

    mine = pl.ds(pl.multiple_of(win * PW, PW), PW)

    def spread(u):
        def one(k, _):
            dst = lax.rem(win + k, WIN)
            pltpu.make_async_remote_copy(
                src_ref=send_v.at[u, dst], dst_ref=g.at[0, u, :, mine, :],
                send_sem=a_send.at[u], recv_sem=a_recv.at[u],
                device_id=(chan, dst), device_id_type=MESH,
            ).start()
            return 0

        lax.fori_loop(1, WIN, one, 0)
        g[0, u, :, mine, :] = send_v[u, win]

    def spread_all(u):
        others = g.at[0, u, :, pl.ds(0, DEEP - PW), :]
        return pltpu.make_async_remote_copy(
            src_ref=others, dst_ref=others, send_sem=a_send.at[u], recv_sem=a_recv.at[u],
            device_id=(chan, win), device_id_type=MESH,
        )

    def remote(src, dst, send, recv, place):
        return pltpu.make_async_remote_copy(
            src_ref=src, dst_ref=dst, send_sem=send, recv_sem=recv,
            device_id=(at(place), win), device_id_type=MESH,
        )

    def direct(u):
        return [
            remote(g.at[0, u], g.at[slot, u], d_send.at[u, i], d_recv.at[u, i], place)
            for i, (slot, place) in enumerate(((1, (-1, 0)), (4, (0, -1))))
        ]

    def relay(u):
        moves = (
            (g.at[1, u], g.at[2, u], (-1, 0)),
            (g.at[1, u, 0], g.at[3, u, 0], (0, -1)),
            (g.at[4, u], g.at[5, u], (0, -1)),
            (g.at[4, u, 1], g.at[3, u, 1], (-1, 0)),
        )
        return [
            remote(src, dst, r_send.at[u, i], r_recv.at[u, i], place)
            for i, (src, dst, place) in enumerate(moves)
        ]

    def turn(slot, u):
        a0, a1 = g[slot, u, 0].T, g[slot, u, 1].T
        turned[slot, pl.ds(0, CH), pl.ds(0, DEEP)] = a0
        turned[slot, pl.ds(0, CH), pl.ds(DEEP, DEEP)] = a1
        turned[slot, pl.ds(CH, CH), pl.ds(0, DEEP)] = a1
        turned[slot, pl.ds(CH, CH), pl.ds(DEEP, DEEP)] = -a0

    def add_product(group, u, lhs, right):
        rhs = jnp.concatenate([g[s, u].reshape(2 * DEEP, CH) for s in right], axis=1)
        part = jnp.dot(turned[lhs], rhs, preferred_element_type=F32)
        acc[group, :, pl.ds(0, CH * len(right))] += part

    def result(group, i):
        return acc[group, :, pl.ds(i * CH, CH)] * SCALE

    def column(place):
        return pl.ds(pl.multiple_of(at(place) * CH, CH), CH)

    def keep(b, place, value):
        for k in range(2):
            out[b, k, :, column(place)] = value[k * CH : (k + 1) * CH]

    def send(b, m, slot, place):
        remote(
            res_send.at[b, m], res_recv.at[b, slot], s_send.at[b, m], s_recv.at[b, slot], place
        ).start()

    def give(b, m, slot, place, value):
        res_send[b, m] = value.astype(BF16)
        pl.when(b == BINS - 1)(lambda: send(b, m, slot, place))

    def give_turned(b, m, slot, place, value):
        res_send[b, m, pl.ds(0, CH), :] = value[:CH].T.astype(BF16)
        res_send[b, m, pl.ds(CH, CH), :] = (-value[CH:]).T.astype(BF16)
        pl.when(b == BINS - 1)(lambda: send(b, m, slot, place))

    half = lax.div(x, 2)

    def compute(u):
        b, q = lax.div(u, PARTS), lax.rem(u, PARTS)
        last = q == PARTS - 1
        for slot in range(3):
            turn(slot, u)

        @pl.when(b == half)
        def _():
            add_product(4, u, 2, (4, 5))

        @pl.when(b != half)
        def _():
            add_product(4, u, 2, (4,))

        @pl.when(last)
        def _():
            @pl.when(b == half)
            def _():
                v = result(4, 1)
                give(b, 9, 9, (2, 0), v)
                give_turned(b, 10, 9, (0, 2), v)

            v = result(4, 0)
            give(b, 5, 5, (2, 0), v)
            give_turned(b, 6, 6, (0, 1), v)

        add_product(3, u, 1, (4, 5))

        @pl.when(last)
        def _():
            v = result(3, 1)
            give_turned(b, 7, 7, (0, 2), v)
            give(b, 8, 8, (1, 0), v)
            v = result(3, 0)
            give(b, 3, 3, (1, 0), v)
            give_turned(b, 4, 4, (0, 1), v)

        add_product(1, u, 0, (2, 3))

        @pl.when(last)
        def _():
            v = result(1, 1)
            give_turned(b, 2, 2, (1, 1), v)
            keep(b, (1, 1), v)
            keep(b, (2, 0), result(1, 0))

        add_product(0, u, 0, (0, 1))

        @pl.when(last)
        def _():
            v = result(0, 1)
            give_turned(b, 0, 0, (1, 0), v)
            keep(b, (1, 0), v)
            keep(b, (0, 0), result(0, 0))

        add_product(2, u, 0, (4, 5))

        @pl.when(last)
        def _():
            v = result(2, 0)
            give_turned(b, 1, 1, (0, 1), v)
            keep(b, (0, 1), v)
            keep(b, (0, 2), result(2, 1))
            acc[...] = jnp.zeros_like(acc)

    def send_first():
        for m, place in enumerate(
            ((1, 0), (0, 1), (1, 1), (1, 0), (0, 1), (2, 0), (0, 1), (0, 2), (1, 0))
        ):
            send(0, m, m, place)

        @pl.when(half == 0)
        def _():
            send(0, 9, 9, (2, 0))
            send(0, 10, 9, (0, 2))

    def take(b):
        for slot, place in enumerate(FOREIGN):
            remote(
                res_recv.at[b, slot], res_recv.at[b, slot], s_send.at[b, slot], s_recv.at[b, slot], (0, 0)
            ).wait_recv()
            keep(b, place, res_recv[b, slot].astype(F32))

    acc[...] = jnp.zeros_like(acc)
    loads[0].wait()
    loads[1].wait()
    whiten(0)
    pl.semaphore_wait(barrier, WIN - 1 + len(MATES))
    spread(0)
    for q in range(1, PARTS):
        loads[1 + q].wait()
        whiten(q)
    for u in range(1, AHEAD):
        spread(u)

    def step(t, _):
        @pl.when(t < UNITS)
        def _():
            spread_all(t).wait_recv()
            for copy in direct(t):
                copy.start()

        @pl.when(t + AHEAD < UNITS)
        def _():
            spread(t + AHEAD)

        @pl.when((t >= 1) & (t <= UNITS))
        def _():
            here, onward = direct(t - 1), relay(t - 1)
            here[0].wait_recv()
            onward[0].start()
            onward[1].start()
            here[1].wait_recv()
            onward[2].start()
            onward[3].start()

        @pl.when(t >= 2)
        def _():
            for copy in relay(t - 2):
                copy.wait_send()
            pl.when(t == UNITS + 1)(send_first)
            for copy in relay(t - 2):
                copy.wait_recv()
            compute(t - 2)

        return 0

    lax.fori_loop(0, UNITS + 2, step, 0)
    take(0)
    take(1)

    def sent(u, _):
        spread_all(u).wait_send()
        for copy in direct(u):
            copy.wait_send()
        return 0

    lax.fori_loop(0, UNITS, sent, 0)

    def gone(b, m):
        remote(
            res_send.at[b, m], res_send.at[b, m], s_send.at[b, m], s_recv.at[b, 0], (0, 0)
        ).wait_send()

    for b in range(BINS):
        for m in range(9):
            gone(b, m)
    gone(half, 9)
    gone(half, 10)


def body(spectra, quality_mask):
    flat = spectra.reshape(2, LW * FREQ, CH)
    dma = pltpu.SemaphoreType.DMA
    return pl.pallas_call(
        kernel,
        out_shape=pltpu.VMEM((BINS, 2, CH, CH * SIDE * SIDE), F32),
        in_specs=[pl.BlockSpec(memory_space=pltpu.HBM)] * 2,
        out_specs=pl.BlockSpec(memory_space=pltpu.VMEM),
        scratch_shapes=[
            pltpu.VMEM((2, LW * FREQ, CH), F32),
            pltpu.VMEM((LW, CH), jnp.int32),
            pltpu.VMEM((UNITS, WIN, 2, PW, CH), BF16),
            pltpu.VMEM((len(PLACES), UNITS, 2, DEEP, CH), BF16),
            pltpu.VMEM((3, 2 * CH, 2 * DEEP), BF16),
            pltpu.VMEM((5, 2 * CH, 2 * CH), F32),
            pltpu.VMEM((BINS, 11, 2 * CH, CH), BF16),
            pltpu.VMEM((BINS, 10, 2 * CH, CH), BF16),
            dma((PARTS + 1,)),
            dma((UNITS,)),
            dma((UNITS,)),
            dma((UNITS, 2)),
            dma((UNITS, 2)),
            dma((UNITS, 4)),
            dma((UNITS, 4)),
            dma((BINS, 11)),
            dma((BINS, 10)),
        ],
        compiler_params=pltpu.CompilerParams(
            collective_id=0, has_side_effects=True, vmem_limit_bytes=40 * 1024 * 1024
        ),
        cost_estimate=pl.CostEstimate(
            flops=5_200_000_000, bytes_accessed=6 * 1024 * 1024, transcendentals=0
        ),
    )(*(pltpu.with_memory_space_constraint(a, pltpu.HBM) for a in (flat, quality_mask)))


def solution(mesh):
    placed = (P(None, "win", None, "chan"), P("win", "chan"))
    return jax.shard_map(
        body, mesh=mesh, in_specs=placed, out_specs=P("win", None, "chan", None), check_vma=False
    )
```

```python
import jax
import jax.numpy as jnp
from jax import lax
from jax.experimental import pallas as pl
from jax.experimental.pallas import tpu as pltpu
from jax.sharding import PartitionSpec as P

MESH = pl.DeviceIdType.MESH
F32, BF16 = jnp.float32, jnp.bfloat16

WIN = 16
SIDE = 4
BINS = 2
FREQ = WIN * BINS
CH = 128
LW = 64
PARTS = 4
PW = LW // PARTS
AHEAD = 2
EARLY, LATE = 1, 4
SEND_NEAR, SEND_FAR = 9, 9
UNITS = BINS * PARTS
DEEP = WIN * PW
ROWS = PW * FREQ
SCALE = 1.0 / 32.0

PLACES = ((0, 0), (1, 0), (2, 0), (1, 1), (0, 1), (0, 2))
FOREIGN = ((-1, 0), (0, -1), (-1, -1), (-1, 1), (1, -1), (-2, 1), (2, -1), (1, -2), (-1, 2), (2, 2))
MATES = ((1, 0), (-1, 0), (2, 0), (0, 1), (0, -1), (0, 2), (1, 1), (-1, -1))


def kernel(
    spec, mask_hbm, out,
    spec_v, mask, send_v, g, turned, turned_far, acc, res_send, res_recv,
    in_sem, a_send, a_recv, d_send, d_recv, r_send, r_recv, s_send, s_recv,
):
    chan, win = lax.axis_index("chan"), lax.axis_index("win")
    x, y = lax.rem(chan, SIDE), lax.div(chan, SIDE)
    way = 1 - 2 * lax.rem(win, 2)

    def at(place):
        dx, dy = place
        return lax.rem(y + way * dy + 2 * SIDE, SIDE) * SIDE + lax.rem(x + way * dx + 2 * SIDE, SIDE)

    barrier = pltpu.get_barrier_semaphore()

    def greet(k, _):
        pl.semaphore_signal(
            barrier, inc=1, device_id=(chan, lax.rem(win + k, WIN)), device_id_type=MESH
        )
        return 0

    lax.fori_loop(1, WIN, greet, 0)
    for place in MATES:
        pl.semaphore_signal(barrier, inc=1, device_id=(at(place), win), device_id_type=MESH)

    loads = [pltpu.make_async_copy(mask_hbm, mask, in_sem.at[PARTS])]
    for q in range(PARTS):
        rows = pl.ds(q * ROWS, ROWS)
        loads.append(pltpu.make_async_copy(spec.at[:, rows, :], spec_v.at[:, rows, :], in_sem.at[q]))
    for load in loads:
        load.start()

    def whiten(q):
        def add(f, total):
            for p in range(2):
                v = spec_v[p, pl.ds(q * ROWS + f, PW, stride=FREQ), :]
                total = total + v * v
            return total

        total = lax.fori_loop(0, FREQ, add, jnp.zeros((PW, CH), F32))
        rms = jnp.sqrt(total * (1.0 / (2 * FREQ)) + 1e-6)
        factor = mask[pl.ds(q * PW, PW), :].astype(F32) / rms

        def scale(dst, _):
            for b in range(BINS):
                for p in range(2):
                    v = spec_v[p, pl.ds(q * ROWS + dst * BINS + b, PW, stride=FREQ), :]
                    send_v[b * PARTS + q, dst, p] = (v * factor).astype(BF16)
            return 0

        lax.fori_loop(0, WIN, scale, 0)

    mine = pl.ds(pl.multiple_of(win * PW, PW), PW)

    def spread(u):
        def one(k, _):
            dst = lax.rem(win + k, WIN)
            pltpu.make_async_remote_copy(
                src_ref=send_v.at[u, dst], dst_ref=g.at[0, u, :, mine, :],
                send_sem=a_send.at[u], recv_sem=a_recv.at[u],
                device_id=(chan, dst), device_id_type=MESH,
            ).start()
            return 0

        lax.fori_loop(1, WIN, one, 0)
        g[0, u, :, mine, :] = send_v[u, win]

    def spread_all(u):
        others = g.at[0, u, :, pl.ds(0, DEEP - PW), :]
        return pltpu.make_async_remote_copy(
            src_ref=others, dst_ref=others, send_sem=a_send.at[u], recv_sem=a_recv.at[u],
            device_id=(chan, win), device_id_type=MESH,
        )

    def remote(src, dst, send, recv, place):
        return pltpu.make_async_remote_copy(
            src_ref=src, dst_ref=dst, send_sem=send, recv_sem=recv,
            device_id=(at(place), win), device_id_type=MESH,
        )

    def direct(u):
        return [
            remote(g.at[0, u], g.at[slot, u], d_send.at[u, i], d_recv.at[u, i], place)
            for i, (slot, place) in enumerate(((1, (-1, 0)), (4, (0, -1))))
        ]

    def relay(u):
        moves = (
            (g.at[1, u], g.at[2, u], (-1, 0)),
            (g.at[1, u, 0], g.at[3, u, 0], (0, -1)),
            (g.at[4, u], g.at[5, u], (0, -1)),
            (g.at[4, u, 1], g.at[3, u, 1], (-1, 0)),
        )
        return [
            remote(src, dst, r_send.at[u, i], r_recv.at[u, i], place)
            for i, (src, dst, place) in enumerate(moves)
        ]

    def turn(slot, u, dst):
        a0, a1 = g[slot, u, 0].T, g[slot, u, 1].T
        dst[pl.ds(0, CH), pl.ds(0, DEEP)] = a0
        dst[pl.ds(0, CH), pl.ds(DEEP, DEEP)] = a1
        dst[pl.ds(CH, CH), pl.ds(0, DEEP)] = a1
        dst[pl.ds(CH, CH), pl.ds(DEEP, DEEP)] = -a0

    def add_product(group, at_col, u, lhs, right):
        rhs = [g[s, u].reshape(2 * DEEP, CH) for s in right]
        rhs = rhs[0] if len(rhs) == 1 else jnp.concatenate(rhs, axis=1)
        left = turned_far[...] if lhs == 2 else turned[u, lhs]
        part = jnp.dot(left, rhs, preferred_element_type=F32)
        acc[group, :, pl.ds(at_col * CH, CH * len(right))] += part

    def result(group, i):
        return acc[group, :, pl.ds(i * CH, CH)] * SCALE

    def column(place):
        return pl.ds(pl.multiple_of(at(place) * CH, CH), CH)

    def keep(b, place, value):
        for k in range(2):
            out[b, k, :, column(place)] = value[k * CH : (k + 1) * CH]

    def send(b, m, slot, place):
        remote(
            res_send.at[b, m], res_recv.at[b, slot], s_send.at[b, m], s_recv.at[b, slot], place
        ).start()

    def give(b, m, value):
        res_send[b, m] = value.astype(BF16)

    def give_turned(b, m, value):
        res_send[b, m, pl.ds(0, CH), :] = value[:CH].T.astype(BF16)
        res_send[b, m, pl.ds(CH, CH), :] = (-value[CH:]).T.astype(BF16)

    half = lax.div(x, 2)

    def early(u):
        b, q = lax.div(u, PARTS), lax.rem(u, PARTS)
        turn(0, u, turned.at[u, 0])
        turn(1, u, turned.at[u, 1])
        add_product(2, 0, u, 1, (4,))
        add_product(0, 0, u, 0, (0, 1))
        add_product(1, 0, u, 0, (4,))

        @pl.when(q == PARTS - 1)
        def _():
            v = result(2, 0)
            give(b, 3, v)
            give_turned(b, 4, v)
            v = result(0, 1)
            give_turned(b, 0, v)
            keep(b, (1, 0), v)
            v = result(1, 0)
            give_turned(b, 1, v)
            keep(b, (0, 1), v)
            keep(b, (0, 0), result(0, 0))
            acc[0] = jnp.zeros_like(acc[0])
            for group in (1, 2):
                acc[group, :, pl.ds(0, CH)] = jnp.zeros((2 * CH, CH), F32)

    def send_early(b):
        for m, place in ((3, (1, 0)), (4, (0, 1)), (0, (1, 0)), (1, (0, 1))):
            send(b, m, m, place)

    def send_far(b):
        send(b, 5, 5, (2, 0))
        send(b, 6, 6, (0, 1))

    def send_both(b):
        send(b, 9, 9, (2, 0))
        send(b, 10, 9, (0, 2))

    def send_side(b):
        send(b, 7, 7, (0, 2))
        send(b, 8, 8, (1, 0))

    def send_diagonal(b):
        send(b, 2, 2, (1, 1))

    def late(u):
        b, q = lax.div(u, PARTS), lax.rem(u, PARTS)
        done = q == PARTS - 1
        now = done & (b == BINS - 1)
        turn(2, u, turned_far)

        @pl.when(b == half)
        def _():
            add_product(4, 0, u, 2, (4, 5))

        @pl.when(b != half)
        def _():
            add_product(4, 0, u, 2, (4,))

        @pl.when(done)
        def _():
            @pl.when(b == half)
            def _():
                v = result(4, 1)
                give(b, 9, v)
                give_turned(b, 10, v)
                pl.when(now)(lambda: send_both(b))

            v = result(4, 0)
            give(b, 5, v)
            give_turned(b, 6, v)
            pl.when(now)(lambda: send_far(b))

        add_product(2, 1, u, 1, (5,))

        @pl.when(done)
        def _():
            v = result(2, 1)
            give_turned(b, 7, v)
            give(b, 8, v)
            pl.when(now)(lambda: send_side(b))

        add_product(3, 0, u, 0, (2, 3))

        @pl.when(done)
        def _():
            v = result(3, 1)
            give_turned(b, 2, v)
            pl.when(now)(lambda: send_diagonal(b))
            keep(b, (1, 1), v)
            keep(b, (2, 0), result(3, 0))

        add_product(1, 1, u, 0, (5,))

        @pl.when(done)
        def _():
            keep(b, (0, 2), result(1, 1))
            for group in (1, 2):
                acc[group, :, pl.ds(CH, CH)] = jnp.zeros((2 * CH, CH), F32)
            for group in (3, 4):
                acc[group] = jnp.zeros_like(acc[group])

    def take(b):
        for slot, place in enumerate(FOREIGN):
            remote(
                res_recv.at[b, slot], res_recv.at[b, slot], s_send.at[b, slot], s_recv.at[b, slot], (0, 0)
            ).wait_recv()
            keep(b, place, res_recv[b, slot].astype(F32))

    acc[...] = jnp.zeros_like(acc)
    loads[0].wait()
    loads[1].wait()
    whiten(0)
    pl.semaphore_wait(barrier, WIN - 1 + len(MATES))
    spread(0)
    for q in range(1, PARTS):
        loads[1 + q].wait()
        whiten(q)
    for u in range(1, AHEAD):
        spread(u)

    def step(t, _):
        @pl.when(t < UNITS)
        def _():
            spread_all(t).wait_recv()
            for copy in direct(t):
                copy.start()

        @pl.when(t + AHEAD < UNITS)
        def _():
            spread(t + AHEAD)

        @pl.when((t >= 1) & (t <= UNITS))
        def _():
            here, onward = direct(t - 1), relay(t - 1)
            here[0].wait_recv()
            onward[0].start()
            onward[1].start()
            here[1].wait_recv()
            onward[2].start()
            onward[3].start()

        @pl.when((t >= EARLY) & (t < UNITS + EARLY))
        def _():
            early(t - EARLY)

        pl.when(t == SEND_NEAR)(lambda: send_early(0))

        @pl.when(t == UNITS + 1)
        def _():
            for copy in relay(UNITS - 1):
                copy.wait_send()
            send_early(1)

        @pl.when(t == SEND_FAR)
        def _():
            send_far(0)
            send_side(0)
            send_diagonal(0)
            pl.when(half == 0)(lambda: send_both(0))

        @pl.when(t >= LATE)
        def _():
            for copy in relay(t - LATE):
                copy.wait_recv()
            late(t - LATE)

        return 0

    lax.fori_loop(0, UNITS + LATE, step, 0)
    take(0)

    def sent(u, _):
        spread_all(u).wait_send()
        for copy in direct(u):
            copy.wait_send()

        @pl.when(u < UNITS - 1)
        def _():
            for copy in relay(u):
                copy.wait_send()

        return 0

    lax.fori_loop(0, UNITS, sent, 0)

    def gone(b, m):
        remote(
            res_send.at[b, m], res_send.at[b, m], s_send.at[b, m], s_recv.at[b, 0], (0, 0)
        ).wait_send()

    for m in range(9):
        gone(0, m)
    pl.when(half == 0)(lambda: (gone(0, 9), gone(0, 10), None)[2])
    take(1)
    for m in range(9):
        gone(1, m)
    pl.when(half == 1)(lambda: (gone(1, 9), gone(1, 10), None)[2])


def body(spectra, quality_mask):
    flat = spectra.reshape(2, LW * FREQ, CH)
    dma = pltpu.SemaphoreType.DMA
    return pl.pallas_call(
        kernel,
        out_shape=pltpu.VMEM((BINS, 2, CH, CH * SIDE * SIDE), F32),
        in_specs=[pl.BlockSpec(memory_space=pltpu.HBM)] * 2,
        out_specs=pl.BlockSpec(memory_space=pltpu.VMEM),
        scratch_shapes=[
            pltpu.VMEM((2, LW * FREQ, CH), F32),
            pltpu.VMEM((LW, CH), jnp.int32),
            pltpu.VMEM((UNITS, WIN, 2, PW, CH), BF16),
            pltpu.VMEM((len(PLACES), UNITS, 2, DEEP, CH), BF16),
            pltpu.VMEM((UNITS, 2, 2 * CH, 2 * DEEP), BF16),
            pltpu.VMEM((2 * CH, 2 * DEEP), BF16),
            pltpu.VMEM((5, 2 * CH, 2 * CH), F32),
            pltpu.VMEM((BINS, 11, 2 * CH, CH), BF16),
            pltpu.VMEM((BINS, 10, 2 * CH, CH), BF16),
            dma((PARTS + 1,)),
            dma((UNITS,)),
            dma((UNITS,)),
            dma((UNITS, 2)),
            dma((UNITS, 2)),
            dma((UNITS, 4)),
            dma((UNITS, 4)),
            dma((BINS, 11)),
            dma((BINS, 10)),
        ],
        compiler_params=pltpu.CompilerParams(
            collective_id=0, has_side_effects=True, vmem_limit_bytes=40 * 1024 * 1024
        ),
        cost_estimate=pl.CostEstimate(
            flops=5_200_000_000, bytes_accessed=6 * 1024 * 1024, transcendentals=0
        ),
    )(*(pltpu.with_memory_space_constraint(a, pltpu.HBM) for a in (flat, quality_mask)))


def solution(mesh):
    placed = (P(None, "win", None, "chan"), P("win", "chan"))
    return jax.shard_map(
        body, mesh=mesh, in_specs=placed, out_specs=P("win", None, "chan", None), check_vma=False
    )
```

```python
import jax
import jax.numpy as jnp
from jax import lax
from jax.experimental import pallas as pl
from jax.experimental.pallas import tpu as pltpu
from jax.sharding import PartitionSpec as P

MESH = pl.DeviceIdType.MESH
F32, BF16 = jnp.float32, jnp.bfloat16

WIN = 16
SIDE = 4
BINS = 2
FREQ = WIN * BINS
CH = 128
LW = 64
PARTS = 4
PW = LW // PARTS
AHEAD = 2
EARLY, LATE = 1, 4
SEND_NEAR, SEND_FAR = 9, 9
UNITS = BINS * PARTS
DEEP = WIN * PW
ROWS = PW * FREQ
SCALE = 1.0 / 32.0

PLACES = ((0, 0), (1, 0), (2, 0), (1, 1), (0, 1), (0, 2))
FOREIGN = ((-1, 0), (0, -1), (-1, -1), (-1, 1), (1, -1), (-2, 1), (2, -1), (1, -2), (-1, 2), (2, 2))
MATES = ((1, 0), (-1, 0), (2, 0), (0, 1), (0, -1), (0, 2), (1, 1), (-1, -1))


def kernel(
    spec, mask_hbm, out,
    spec_v, mask, send_v, g, turned, turned_far, acc, res_send, res_recv,
    in_sem, a_send, a_recv, d_send, d_recv, r_send, r_recv, s_send, s_recv,
):
    chan, win = lax.axis_index("chan"), lax.axis_index("win")
    x, y = lax.rem(chan, SIDE), lax.div(chan, SIDE)
    way = 1 - 2 * lax.rem(win, 2)

    def at(place):
        dx, dy = place
        return lax.rem(y + way * dy + 2 * SIDE, SIDE) * SIDE + lax.rem(x + way * dx + 2 * SIDE, SIDE)

    loads = [pltpu.make_async_copy(mask_hbm, mask, in_sem.at[PARTS])]
    for q in range(PARTS):
        rows = pl.ds(q * ROWS, ROWS)
        loads.append(pltpu.make_async_copy(spec.at[:, rows, :], spec_v.at[:, rows, :], in_sem.at[q]))
    for load in loads:
        load.start()

    barrier = pltpu.get_barrier_semaphore()

    def greet(k, _):
        pl.semaphore_signal(
            barrier, inc=1, device_id=(chan, lax.rem(win + k, WIN)), device_id_type=MESH
        )
        return 0

    lax.fori_loop(1, WIN, greet, 0)
    for place in MATES:
        pl.semaphore_signal(barrier, inc=1, device_id=(at(place), win), device_id_type=MESH)

    def whiten(q):
        def add(f, total):
            for p in range(2):
                v = spec_v[p, pl.ds(q * ROWS + f, PW, stride=FREQ), :]
                total = total + v * v
            return total

        total = lax.fori_loop(0, FREQ, add, jnp.zeros((PW, CH), F32), unroll=8)
        rms = jnp.sqrt(total * (1.0 / (2 * FREQ)) + 1e-6)
        factor = mask[pl.ds(q * PW, PW), :].astype(F32) / rms

        def scale(dst, _):
            for b in range(BINS):
                for p in range(2):
                    v = spec_v[p, pl.ds(q * ROWS + dst * BINS + b, PW, stride=FREQ), :]
                    send_v[b * PARTS + q, dst, p] = (v * factor).astype(BF16)
            return 0

        lax.fori_loop(0, WIN, scale, 0, unroll=4)

    mine = pl.ds(pl.multiple_of(win * PW, PW), PW)

    def spread(u):
        def one(k, _):
            apart = WIN // 2 + lax.div(k + 1, 2) * (1 - 2 * lax.rem(k, 2))
            dst = lax.rem(win + apart, WIN)
            pltpu.make_async_remote_copy(
                src_ref=send_v.at[u, dst], dst_ref=g.at[0, u, :, mine, :],
                send_sem=a_send.at[u], recv_sem=a_recv.at[u],
                device_id=(chan, dst), device_id_type=MESH,
            ).start()
            return 0

        lax.fori_loop(0, WIN - 1, one, 0)
        g[0, u, :, mine, :] = send_v[u, win]

    def spread_all(u):
        others = g.at[0, u, :, pl.ds(0, DEEP - PW), :]
        return pltpu.make_async_remote_copy(
            src_ref=others, dst_ref=others, send_sem=a_send.at[u], recv_sem=a_recv.at[u],
            device_id=(chan, win), device_id_type=MESH,
        )

    def remote(src, dst, send, recv, place):
        return pltpu.make_async_remote_copy(
            src_ref=src, dst_ref=dst, send_sem=send, recv_sem=recv,
            device_id=(at(place), win), device_id_type=MESH,
        )

    def direct(u):
        return [
            remote(g.at[0, u], g.at[slot, u], d_send.at[u, i], d_recv.at[u, i], place)
            for i, (slot, place) in enumerate(((1, (-1, 0)), (4, (0, -1))))
        ]

    def relay(u):
        moves = (
            (g.at[1, u], g.at[2, u], (-1, 0)),
            (g.at[1, u, 0], g.at[3, u, 0], (0, -1)),
            (g.at[4, u], g.at[5, u], (0, -1)),
            (g.at[4, u, 1], g.at[3, u, 1], (-1, 0)),
        )
        return [
            remote(src, dst, r_send.at[u, i], r_recv.at[u, i], place)
            for i, (src, dst, place) in enumerate(moves)
        ]

    def turn(slot, u, dst):
        a0, a1 = g[slot, u, 0].T, g[slot, u, 1].T
        dst[pl.ds(0, CH), pl.ds(0, DEEP)] = a0
        dst[pl.ds(0, CH), pl.ds(DEEP, DEEP)] = a1
        dst[pl.ds(CH, CH), pl.ds(0, DEEP)] = a1
        dst[pl.ds(CH, CH), pl.ds(DEEP, DEEP)] = -a0

    def add_product(group, at_col, u, lhs, right):
        rhs = [g[s, u].reshape(2 * DEEP, CH) for s in right]
        rhs = rhs[0] if len(rhs) == 1 else jnp.concatenate(rhs, axis=1)
        left = turned_far[...] if lhs == 2 else turned[u, lhs]
        part = jnp.dot(left, rhs, preferred_element_type=F32)
        acc[group, :, pl.ds(at_col * CH, CH * len(right))] += part

    def result(group, i):
        return acc[group, :, pl.ds(i * CH, CH)] * SCALE

    def column(place):
        return pl.ds(pl.multiple_of(at(place) * CH, CH), CH)

    def keep(b, place, value):
        for k in range(2):
            out[b, k, :, column(place)] = value[k * CH : (k + 1) * CH]

    def send(b, m, slot, place):
        remote(
            res_send.at[b, m], res_recv.at[b, slot], s_send.at[b, m], s_recv.at[b, slot], place
        ).start()

    def give(b, m, value):
        res_send[b, m] = value.astype(BF16)

    def give_turned(b, m, value):
        res_send[b, m, pl.ds(0, CH), :] = value[:CH].T.astype(BF16)
        res_send[b, m, pl.ds(CH, CH), :] = (-value[CH:]).T.astype(BF16)

    half = lax.div(x, 2)

    def early(u):
        b, q = lax.div(u, PARTS), lax.rem(u, PARTS)
        turn(0, u, turned.at[u, 0])
        turn(1, u, turned.at[u, 1])
        add_product(2, 0, u, 1, (4,))
        add_product(0, 0, u, 0, (0, 1))
        add_product(1, 0, u, 0, (4,))

        @pl.when(q == PARTS - 1)
        def _():
            v = result(2, 0)
            give(b, 3, v)
            give_turned(b, 4, v)
            v = result(0, 1)
            give_turned(b, 0, v)
            keep(b, (1, 0), v)
            v = result(1, 0)
            give_turned(b, 1, v)
            keep(b, (0, 1), v)
            keep(b, (0, 0), result(0, 0))
            acc[0] = jnp.zeros_like(acc[0])
            for group in (1, 2):
                acc[group, :, pl.ds(0, CH)] = jnp.zeros((2 * CH, CH), F32)

    def send_early(b):
        for m, place in ((3, (1, 0)), (4, (0, 1)), (0, (1, 0)), (1, (0, 1))):
            send(b, m, m, place)

    def send_far(b):
        send(b, 5, 5, (2, 0))
        send(b, 6, 6, (0, 1))

    def send_both(b):
        send(b, 9, 9, (2, 0))
        send(b, 10, 9, (0, 2))

    def send_side(b):
        send(b, 7, 7, (0, 2))
        send(b, 8, 8, (1, 0))

    def send_diagonal(b):
        send(b, 2, 2, (1, 1))

    def late(u):
        b, q = lax.div(u, PARTS), lax.rem(u, PARTS)
        done = q == PARTS - 1
        now = done & (b == BINS - 1)
        turn(2, u, turned_far)

        @pl.when(b == half)
        def _():
            add_product(4, 0, u, 2, (4, 5))

        @pl.when(b != half)
        def _():
            add_product(4, 0, u, 2, (4,))

        @pl.when(done)
        def _():
            @pl.when(b == half)
            def _():
                v = result(4, 1)
                give(b, 9, v)
                give_turned(b, 10, v)
                pl.when(now)(lambda: send_both(b))

            v = result(4, 0)
            give(b, 5, v)
            give_turned(b, 6, v)
            pl.when(now)(lambda: send_far(b))

        add_product(2, 1, u, 1, (5,))

        @pl.when(done)
        def _():
            v = result(2, 1)
            give_turned(b, 7, v)
            give(b, 8, v)
            pl.when(now)(lambda: send_side(b))

        add_product(3, 0, u, 0, (2, 3))

        @pl.when(done)
        def _():
            v = result(3, 1)
            give_turned(b, 2, v)
            pl.when(now)(lambda: send_diagonal(b))
            keep(b, (1, 1), v)
            keep(b, (2, 0), result(3, 0))

        add_product(1, 1, u, 0, (5,))

        @pl.when(done)
        def _():
            keep(b, (0, 2), result(1, 1))
            for group in (1, 2):
                acc[group, :, pl.ds(CH, CH)] = jnp.zeros((2 * CH, CH), F32)
            for group in (3, 4):
                acc[group] = jnp.zeros_like(acc[group])

    def take(b):
        for slot in (3, 4, 0, 1, 9, 5, 6, 7, 8, 2):
            place = FOREIGN[slot]
            remote(
                res_recv.at[b, slot], res_recv.at[b, slot], s_send.at[b, slot], s_recv.at[b, slot], (0, 0)
            ).wait_recv()
            keep(b, place, res_recv[b, slot].astype(F32))

    loads[0].wait()
    loads[1].wait()
    whiten(0)
    pl.semaphore_wait(barrier, WIN - 1 + len(MATES))
    spread(0)
    acc[...] = jnp.zeros_like(acc)
    for q in range(1, PARTS):
        loads[1 + q].wait()
        whiten(q)
    for u in range(1, AHEAD):
        spread(u)

    def step(t, _):
        @pl.when(t < UNITS)
        def _():
            spread_all(t).wait_recv()
            for copy in direct(t):
                copy.start()

        @pl.when(t + AHEAD < UNITS)
        def _():
            spread(t + AHEAD)

        @pl.when((t >= 1) & (t <= UNITS))
        def _():
            here, onward = direct(t - 1), relay(t - 1)
            here[0].wait_recv()
            onward[0].start()
            onward[1].start()
            here[1].wait_recv()
            onward[2].start()
            onward[3].start()

        @pl.when((t >= EARLY) & (t < UNITS + EARLY))
        def _():
            early(t - EARLY)

        pl.when(t == SEND_NEAR)(lambda: send_early(0))

        @pl.when(t == UNITS + 1)
        def _():
            for copy in relay(UNITS - 1):
                copy.wait_send()
            send_early(1)

        @pl.when(t == SEND_FAR)
        def _():
            send_far(0)
            send_side(0)
            send_diagonal(0)
            pl.when(half == 0)(lambda: send_both(0))

        @pl.when(t >= LATE)
        def _():
            for copy in relay(t - LATE):
                copy.wait_recv()
            late(t - LATE)

        return 0

    lax.fori_loop(0, UNITS + LATE, step, 0)
    take(0)

    def sent(u, _):
        spread_all(u).wait_send()
        for copy in direct(u):
            copy.wait_send()

        @pl.when(u < UNITS - 1)
        def _():
            for copy in relay(u):
                copy.wait_send()

        return 0

    lax.fori_loop(0, UNITS, sent, 0)

    def gone(b, m):
        remote(
            res_send.at[b, m], res_send.at[b, m], s_send.at[b, m], s_recv.at[b, 0], (0, 0)
        ).wait_send()

    for m in range(9):
        gone(0, m)
    pl.when(half == 0)(lambda: (gone(0, 9), gone(0, 10), None)[2])
    take(1)
    for m in range(9):
        gone(1, m)
    pl.when(half == 1)(lambda: (gone(1, 9), gone(1, 10), None)[2])


def body(spectra, quality_mask):
    flat = spectra.reshape(2, LW * FREQ, CH)
    dma = pltpu.SemaphoreType.DMA
    return pl.pallas_call(
        kernel,
        out_shape=pltpu.VMEM((BINS, 2, CH, CH * SIDE * SIDE), F32),
        in_specs=[pl.BlockSpec(memory_space=pltpu.HBM)] * 2,
        out_specs=pl.BlockSpec(memory_space=pltpu.VMEM),
        scratch_shapes=[
            pltpu.VMEM((2, LW * FREQ, CH), F32),
            pltpu.VMEM((LW, CH), jnp.int32),
            pltpu.VMEM((UNITS, WIN, 2, PW, CH), BF16),
            pltpu.VMEM((len(PLACES), UNITS, 2, DEEP, CH), BF16),
            pltpu.VMEM((UNITS, 2, 2 * CH, 2 * DEEP), BF16),
            pltpu.VMEM((2 * CH, 2 * DEEP), BF16),
            pltpu.VMEM((5, 2 * CH, 2 * CH), F32),
            pltpu.VMEM((BINS, 11, 2 * CH, CH), BF16),
            pltpu.VMEM((BINS, 10, 2 * CH, CH), BF16),
            dma((PARTS + 1,)),
            dma((UNITS,)),
            dma((UNITS,)),
            dma((UNITS, 2)),
            dma((UNITS, 2)),
            dma((UNITS, 4)),
            dma((UNITS, 4)),
            dma((BINS, 11)),
            dma((BINS, 10)),
        ],
        compiler_params=pltpu.CompilerParams(
            collective_id=0, has_side_effects=True, vmem_limit_bytes=40 * 1024 * 1024
        ),
        cost_estimate=pl.CostEstimate(
            flops=5_200_000_000, bytes_accessed=6 * 1024 * 1024, transcendentals=0
        ),
    )(*(pltpu.with_memory_space_constraint(a, pltpu.HBM) for a in (flat, quality_mask)))


def solution(mesh):
    placed = (P(None, "win", None, "chan"), P("win", "chan"))
    return jax.shard_map(
        body, mesh=mesh, in_specs=placed, out_specs=P("win", None, "chan", None), check_vma=False
    )
```

```python
import jax
import jax.numpy as jnp
from jax import lax
from jax.experimental import pallas as pl
from jax.experimental.pallas import tpu as pltpu
from jax.sharding import PartitionSpec as P

MESH = pl.DeviceIdType.MESH
F32, BF16 = jnp.float32, jnp.bfloat16

WIN = 16
SIDE = 4
BINS = 2
FREQ = WIN * BINS
CH = 128
LW = 64
PARTS = 4
PW = LW // PARTS
AHEAD = 2
EARLY, LATE = 1, 4
SEND_NEAR, SEND_FAR = 9, 9
UNITS = BINS * PARTS
DEEP = WIN * PW
ROWS = PW * FREQ
SCALE = 1.0 / 32.0

PLACES = ((0, 0), (1, 0), (2, 0), (1, 1), (0, 1), (0, 2))
FOREIGN = ((-1, 0), (0, -1), (-1, -1), (-1, 1), (1, -1), (-2, 1), (2, -1), (1, -2), (-1, 2), (2, 2))
MATES = ((1, 0), (-1, 0), (2, 0), (0, 1), (0, -1), (0, 2), (1, 1), (-1, -1))


def kernel(
    spec, mask_hbm, out,
    spec_v, mask, send_v, g, turned, turned_far, acc, res_send, res_recv,
    in_sem, a_send, a_recv, d_send, d_recv, r_send, r_recv, s_send, s_recv,
):
    chan, win = lax.axis_index("chan"), lax.axis_index("win")
    x, y = lax.rem(chan, SIDE), lax.div(chan, SIDE)
    way = 1 - 2 * lax.rem(win, 2)

    def at(place):
        dx, dy = place
        return lax.rem(y + way * dy + 2 * SIDE, SIDE) * SIDE + lax.rem(x + way * dx + 2 * SIDE, SIDE)

    loads = [pltpu.make_async_copy(mask_hbm, mask, in_sem.at[PARTS])]
    for q in range(PARTS):
        rows = pl.ds(q * ROWS, ROWS)
        loads.append(pltpu.make_async_copy(spec.at[:, rows, :], spec_v.at[:, rows, :], in_sem.at[q]))
    for load in loads:
        load.start()

    barrier = pltpu.get_barrier_semaphore()

    def greet(k, _):
        pl.semaphore_signal(
            barrier, inc=1, device_id=(chan, lax.rem(win + k, WIN)), device_id_type=MESH
        )
        return 0

    lax.fori_loop(1, WIN, greet, 0)
    for place in MATES:
        pl.semaphore_signal(barrier, inc=1, device_id=(at(place), win), device_id_type=MESH)

    def whiten(q):
        def add(f, total):
            for p in range(2):
                v = spec_v[p, pl.ds(q * ROWS + f, PW, stride=FREQ), :]
                total = total + v * v
            return total

        total = lax.fori_loop(0, FREQ, add, jnp.zeros((PW, CH), F32), unroll=8)
        rms = jnp.sqrt(total * (1.0 / (2 * FREQ)) + 1e-6)
        factor = mask[pl.ds(q * PW, PW), :].astype(F32) / rms

        def scale(dst, _):
            for b in range(BINS):
                for p in range(2):
                    v = spec_v[p, pl.ds(q * ROWS + dst * BINS + b, PW, stride=FREQ), :]
                    send_v[b * PARTS + q, dst, p] = (v * factor).astype(BF16)
            return 0

        lax.fori_loop(0, WIN, scale, 0, unroll=4)

    mine = pl.ds(pl.multiple_of(win * PW, PW), PW)

    def spread(u):
        def one(k, _):
            apart = WIN // 2 + lax.div(k + 1, 2) * (1 - 2 * lax.rem(k, 2))
            dst = lax.rem(win + apart, WIN)
            pltpu.make_async_remote_copy(
                src_ref=send_v.at[u, dst], dst_ref=g.at[0, u, :, mine, :],
                send_sem=a_send.at[u], recv_sem=a_recv.at[u],
                device_id=(chan, dst), device_id_type=MESH,
            ).start()
            return 0

        lax.fori_loop(0, WIN - 1, one, 0)
        g[0, u, :, mine, :] = send_v[u, win]

    def spread_all(u):
        others = g.at[0, u, :, pl.ds(0, DEEP - PW), :]
        return pltpu.make_async_remote_copy(
            src_ref=others, dst_ref=others, send_sem=a_send.at[u], recv_sem=a_recv.at[u],
            device_id=(chan, win), device_id_type=MESH,
        )

    def remote(src, dst, send, recv, place):
        return pltpu.make_async_remote_copy(
            src_ref=src, dst_ref=dst, send_sem=send, recv_sem=recv,
            device_id=(at(place), win), device_id_type=MESH,
        )

    def direct(u):
        return [
            remote(g.at[0, u], g.at[slot, u], d_send.at[u, i], d_recv.at[u, i], place)
            for i, (slot, place) in enumerate(((1, (-1, 0)), (4, (0, -1))))
        ]

    def relay(u):
        moves = (
            (g.at[1, u], g.at[2, u], (-1, 0)),
            (g.at[1, u, 0], g.at[3, u, 0], (0, -1)),
            (g.at[4, u], g.at[5, u], (0, -1)),
            (g.at[4, u, 1], g.at[3, u, 1], (-1, 0)),
        )
        return [
            remote(src, dst, r_send.at[u, i], r_recv.at[u, i], place)
            for i, (src, dst, place) in enumerate(moves)
        ]

    def turn(slot, u, dst):
        a0, a1 = g[slot, u, 0].T, g[slot, u, 1].T
        dst[pl.ds(0, CH), pl.ds(0, DEEP)] = a0
        dst[pl.ds(0, CH), pl.ds(DEEP, DEEP)] = a1
        dst[pl.ds(CH, CH), pl.ds(0, DEEP)] = a1
        dst[pl.ds(CH, CH), pl.ds(DEEP, DEEP)] = -a0

    def add_product(group, at_col, u, lhs, right):
        rhs = [g[s, u].reshape(2 * DEEP, CH) for s in right]
        rhs = rhs[0] if len(rhs) == 1 else jnp.concatenate(rhs, axis=1)
        left = turned_far[...] if lhs == 2 else turned[u, lhs]
        part = jnp.dot(left, rhs, preferred_element_type=F32)
        acc[group, :, pl.ds(at_col * CH, CH * len(right))] += part

    def result(group, i):
        return acc[group, :, pl.ds(i * CH, CH)] * SCALE

    def column(place):
        return pl.ds(pl.multiple_of(at(place) * CH, CH), CH)

    def keep(b, place, value):
        for k in range(2):
            out[b, k, :, column(place)] = value[k * CH : (k + 1) * CH]

    def send(b, m, slot, place):
        remote(
            res_send.at[b, m], res_recv.at[b, slot], s_send.at[b, m], s_recv.at[b, slot], place
        ).start()

    def give(b, m, value):
        res_send[b, m] = value.astype(BF16)

    def give_turned(b, m, value):
        res_send[b, m, pl.ds(0, CH), :] = value[:CH].T.astype(BF16)
        res_send[b, m, pl.ds(CH, CH), :] = (-value[CH:]).T.astype(BF16)

    half = lax.div(x, 2)

    def early(u):
        b, q = lax.div(u, PARTS), lax.rem(u, PARTS)
        turn(0, u, turned.at[u, 0])
        turn(1, u, turned.at[u, 1])
        add_product(2, 0, u, 1, (4,))
        add_product(0, 0, u, 0, (0, 1))
        add_product(1, 0, u, 0, (4,))

        @pl.when(q == PARTS - 1)
        def _():
            v = result(2, 0)
            give(b, 3, v)
            give_turned(b, 4, v)
            v = result(0, 1)
            give_turned(b, 0, v)
            keep(b, (1, 0), v)
            v = result(1, 0)
            give_turned(b, 1, v)
            keep(b, (0, 1), v)
            keep(b, (0, 0), result(0, 0))
            acc[0] = jnp.zeros_like(acc[0])
            for group in (1, 2):
                acc[group, :, pl.ds(0, CH)] = jnp.zeros((2 * CH, CH), F32)

    def send_early(b):
        for m, place in ((3, (1, 0)), (4, (0, 1)), (0, (1, 0)), (1, (0, 1))):
            send(b, m, m, place)

    def send_far(b):
        send(b, 5, 5, (2, 0))
        send(b, 6, 6, (0, 1))

    def send_both(b):
        send(b, 9, 9, (2, 0))
        send(b, 10, 9, (0, 2))

    def send_side(b):
        send(b, 7, 7, (0, 2))
        send(b, 8, 8, (1, 0))

    def send_diagonal(b):
        send(b, 2, 2, (1, 1))

    def late(u):
        b, q = lax.div(u, PARTS), lax.rem(u, PARTS)
        done = q == PARTS - 1
        now = done & (b == BINS - 1)
        turn(2, u, turned_far)

        @pl.when(b == half)
        def _():
            add_product(4, 0, u, 2, (4, 5))

        @pl.when(b != half)
        def _():
            add_product(4, 0, u, 2, (4,))

        @pl.when(done)
        def _():
            @pl.when(b == half)
            def _():
                v = result(4, 1)
                give(b, 9, v)
                give_turned(b, 10, v)
                pl.when(now)(lambda: send_both(b))

            v = result(4, 0)
            give(b, 5, v)
            give_turned(b, 6, v)
            pl.when(now)(lambda: send_far(b))

        add_product(2, 1, u, 1, (5,))

        @pl.when(done)
        def _():
            v = result(2, 1)
            give_turned(b, 7, v)
            give(b, 8, v)
            pl.when(now)(lambda: send_side(b))

        add_product(3, 0, u, 0, (2, 3))

        @pl.when(done)
        def _():
            v = result(3, 1)
            give_turned(b, 2, v)
            pl.when(now)(lambda: send_diagonal(b))
            keep(b, (1, 1), v)
            keep(b, (2, 0), result(3, 0))

        add_product(1, 1, u, 0, (5,))

        @pl.when(done)
        def _():
            keep(b, (0, 2), result(1, 1))
            for group in (1, 2):
                acc[group, :, pl.ds(CH, CH)] = jnp.zeros((2 * CH, CH), F32)
            for group in (3, 4):
                acc[group] = jnp.zeros_like(acc[group])

    def take(b):
        for slot in (3, 4, 0, 1, 9, 5, 6, 7, 8, 2):
            place = FOREIGN[slot]
            remote(
                res_recv.at[b, slot], res_recv.at[b, slot], s_send.at[b, slot], s_recv.at[b, slot], (0, 0)
            ).wait_recv()
            keep(b, place, res_recv[b, slot].astype(F32))

    loads[0].wait()
    loads[1].wait()
    whiten(0)
    pl.semaphore_wait(barrier, WIN - 1 + len(MATES))
    spread(0)
    acc[...] = jnp.zeros_like(acc)
    for q in range(1, PARTS):
        loads[1 + q].wait()
        whiten(q)
    for u in range(1, AHEAD):
        spread(u)

    def step(t, _):
        @pl.when(t < UNITS)
        def _():
            spread_all(t).wait_recv()
            for copy in direct(t):
                copy.start()

        @pl.when(t + AHEAD < UNITS)
        def _():
            spread(t + AHEAD)

        @pl.when((t >= 1) & (t <= UNITS))
        def _():
            here, onward = direct(t - 1), relay(t - 1)
            here[0].wait_recv()
            onward[0].start()
            onward[1].start()
            here[1].wait_recv()
            onward[2].start()
            onward[3].start()

        @pl.when((t >= EARLY) & (t < UNITS + EARLY))
        def _():
            early(t - EARLY)

        pl.when(t == UNITS)(lambda: send_early(1))
        pl.when(t == SEND_NEAR)(lambda: send_early(0))

        @pl.when(t == UNITS + 1)
        def _():
            for copy in relay(UNITS - 1):
                copy.wait_send()

        @pl.when(t == SEND_FAR)
        def _():
            send_far(0)
            send_side(0)
            send_diagonal(0)
            pl.when(half == 0)(lambda: send_both(0))

        @pl.when(t >= LATE)
        def _():
            for copy in relay(t - LATE):
                copy.wait_recv()
            late(t - LATE)

        return 0

    lax.fori_loop(0, UNITS + LATE, step, 0)
    take(0)

    def sent(u, _):
        spread_all(u).wait_send()
        for copy in direct(u):
            copy.wait_send()

        @pl.when(u < UNITS - 1)
        def _():
            for copy in relay(u):
                copy.wait_send()

        return 0

    lax.fori_loop(0, UNITS, sent, 0)

    def gone(b, m):
        remote(
            res_send.at[b, m], res_send.at[b, m], s_send.at[b, m], s_recv.at[b, 0], (0, 0)
        ).wait_send()

    for m in range(9):
        gone(0, m)
    pl.when(half == 0)(lambda: (gone(0, 9), gone(0, 10), None)[2])
    take(1)
    for m in range(9):
        gone(1, m)
    pl.when(half == 1)(lambda: (gone(1, 9), gone(1, 10), None)[2])


def body(spectra, quality_mask):
    flat = spectra.reshape(2, LW * FREQ, CH)
    dma = pltpu.SemaphoreType.DMA
    return pl.pallas_call(
        kernel,
        out_shape=pltpu.VMEM((BINS, 2, CH, CH * SIDE * SIDE), F32),
        in_specs=[pl.BlockSpec(memory_space=pltpu.HBM)] * 2,
        out_specs=pl.BlockSpec(memory_space=pltpu.VMEM),
        scratch_shapes=[
            pltpu.VMEM((2, LW * FREQ, CH), F32),
            pltpu.VMEM((LW, CH), jnp.int32),
            pltpu.VMEM((UNITS, WIN, 2, PW, CH), BF16),
            pltpu.VMEM((len(PLACES), UNITS, 2, DEEP, CH), BF16),
            pltpu.VMEM((UNITS, 2, 2 * CH, 2 * DEEP), BF16),
            pltpu.VMEM((2 * CH, 2 * DEEP), BF16),
            pltpu.VMEM((5, 2 * CH, 2 * CH), F32),
            pltpu.VMEM((BINS, 11, 2 * CH, CH), BF16),
            pltpu.VMEM((BINS, 10, 2 * CH, CH), BF16),
            dma((PARTS + 1,)),
            dma((UNITS,)),
            dma((UNITS,)),
            dma((UNITS, 2)),
            dma((UNITS, 2)),
            dma((UNITS, 4)),
            dma((UNITS, 4)),
            dma((BINS, 11)),
            dma((BINS, 10)),
        ],
        compiler_params=pltpu.CompilerParams(
            collective_id=0, has_side_effects=True, vmem_limit_bytes=40 * 1024 * 1024
        ),
        cost_estimate=pl.CostEstimate(
            flops=5_200_000_000, bytes_accessed=6 * 1024 * 1024, transcendentals=0
        ),
    )(*(pltpu.with_memory_space_constraint(a, pltpu.HBM) for a in (flat, quality_mask)))


def solution(mesh):
    placed = (P(None, "win", None, "chan"), P("win", "chan"))
    return jax.shard_map(
        body, mesh=mesh, in_specs=placed, out_specs=P("win", None, "chan", None), check_vma=False
    )
```

```python
import jax
import jax.numpy as jnp
from jax import lax
from jax.experimental import pallas as pl
from jax.experimental.pallas import tpu as pltpu
from jax.sharding import PartitionSpec as P

MESH = pl.DeviceIdType.MESH
F32, BF16 = jnp.float32, jnp.bfloat16

WIN = 16
SIDE = 4
BINS = 2
FREQ = WIN * BINS
CH = 128
LW = 64
PARTS = 4
PW = LW // PARTS
AHEAD = 2
EARLY, LATE = 1, 4
SEND_NEAR, SEND_FAR = 9, 9
UNITS = BINS * PARTS
DEEP = WIN * PW
ROWS = PW * FREQ
SCALE = 1.0 / 32.0

PLACES = ((0, 0), (1, 0), (2, 0), (1, 1), (0, 1), (0, 2))
FOREIGN = ((-1, 0), (0, -1), (-1, -1), (-1, 1), (1, -1), (-2, 1), (2, -1), (1, -2), (-1, 2), (2, 2))
MATES = ((1, 0), (-1, 0), (2, 0), (0, 1), (0, -1), (0, 2), (1, 1), (-1, -1))


def kernel(
    spec, mask_hbm, out,
    spec_v, mask, send_v, g, turned, turned_far, acc, res_send, res_recv,
    in_sem, a_send, a_recv, d_send, d_recv, r_send, r_recv, s_send, s_recv,
):
    chan, win = lax.axis_index("chan"), lax.axis_index("win")
    x, y = lax.rem(chan, SIDE), lax.div(chan, SIDE)
    way = 1 - 2 * lax.rem(win, 2)

    def at(place):
        dx, dy = place
        return lax.rem(y + way * dy + 2 * SIDE, SIDE) * SIDE + lax.rem(x + way * dx + 2 * SIDE, SIDE)

    loads = [pltpu.make_async_copy(mask_hbm, mask, in_sem.at[PARTS])]
    for q in range(PARTS):
        rows = pl.ds(q * ROWS, ROWS)
        loads.append(pltpu.make_async_copy(spec.at[:, rows, :], spec_v.at[:, rows, :], in_sem.at[q]))
    for load in loads:
        load.start()

    barrier = pltpu.get_barrier_semaphore()

    def greet(k, _):
        pl.semaphore_signal(
            barrier, inc=1, device_id=(chan, lax.rem(win + k, WIN)), device_id_type=MESH
        )
        return 0

    lax.fori_loop(1, WIN, greet, 0)
    for place in MATES:
        pl.semaphore_signal(barrier, inc=1, device_id=(at(place), win), device_id_type=MESH)

    def whiten(q):
        def add(f, total):
            for p in range(2):
                v = spec_v[p, pl.ds(q * ROWS + f, PW, stride=FREQ), :]
                total = total + v * v
            return total

        total = lax.fori_loop(0, FREQ, add, jnp.zeros((PW, CH), F32), unroll=8)
        rms = jnp.sqrt(total * (1.0 / (2 * FREQ)) + 1e-6)
        factor = mask[pl.ds(q * PW, PW), :].astype(F32) / rms

        def scale(dst, _):
            for b in range(BINS):
                for p in range(2):
                    v = spec_v[p, pl.ds(q * ROWS + dst * BINS + b, PW, stride=FREQ), :]
                    send_v[b * PARTS + q, dst, p] = (v * factor).astype(BF16)
            return 0

        lax.fori_loop(0, WIN, scale, 0, unroll=4)

    mine = pl.ds(pl.multiple_of(win * PW, PW), PW)

    def spread(u):
        def one(k, _):
            apart = WIN // 2 + lax.div(k + 1, 2) * (1 - 2 * lax.rem(k, 2))
            dst = lax.rem(win + apart, WIN)
            pltpu.make_async_remote_copy(
                src_ref=send_v.at[u, dst], dst_ref=g.at[0, u, :, mine, :],
                send_sem=a_send.at[u], recv_sem=a_recv.at[u],
                device_id=(chan, dst), device_id_type=MESH,
            ).start()
            return 0

        lax.fori_loop(0, WIN - 1, one, 0)
        g[0, u, :, mine, :] = send_v[u, win]

    def spread_all(u):
        others = g.at[0, u, :, pl.ds(0, DEEP - PW), :]
        return pltpu.make_async_remote_copy(
            src_ref=others, dst_ref=others, send_sem=a_send.at[u], recv_sem=a_recv.at[u],
            device_id=(chan, win), device_id_type=MESH,
        )

    def remote(src, dst, send, recv, place):
        return pltpu.make_async_remote_copy(
            src_ref=src, dst_ref=dst, send_sem=send, recv_sem=recv,
            device_id=(at(place), win), device_id_type=MESH,
        )

    def direct(u):
        return [
            remote(g.at[0, u], g.at[slot, u], d_send.at[u, i], d_recv.at[u, i], place)
            for i, (slot, place) in enumerate(((1, (-1, 0)), (4, (0, -1))))
        ]

    def relay(u):
        moves = (
            (g.at[1, u], g.at[2, u], (-1, 0)),
            (g.at[1, u, 0], g.at[3, u, 0], (0, -1)),
            (g.at[4, u], g.at[5, u], (0, -1)),
            (g.at[4, u, 1], g.at[3, u, 1], (-1, 0)),
        )
        return [
            remote(src, dst, r_send.at[u, i], r_recv.at[u, i], place)
            for i, (src, dst, place) in enumerate(moves)
        ]

    def turn(slot, u, dst):
        a0, a1 = g[slot, u, 0].T, g[slot, u, 1].T
        dst[pl.ds(0, CH), pl.ds(0, DEEP)] = a0
        dst[pl.ds(0, CH), pl.ds(DEEP, DEEP)] = a1
        dst[pl.ds(CH, CH), pl.ds(0, DEEP)] = a1
        dst[pl.ds(CH, CH), pl.ds(DEEP, DEEP)] = -a0

    def add_product(group, at_col, u, lhs, right):
        rhs = [g[s, u].reshape(2 * DEEP, CH) for s in right]
        rhs = rhs[0] if len(rhs) == 1 else jnp.concatenate(rhs, axis=1)
        left = turned_far[...] if lhs == 2 else turned[u, lhs]
        part = jnp.dot(left, rhs, preferred_element_type=F32)
        acc[group, :, pl.ds(at_col * CH, CH * len(right))] += part

    def result(group, i):
        return acc[group, :, pl.ds(i * CH, CH)] * SCALE

    def column(place):
        return pl.ds(pl.multiple_of(at(place) * CH, CH), CH)

    def keep(b, place, value):
        for k in range(2):
            out[b, k, :, column(place)] = value[k * CH : (k + 1) * CH]

    def send(b, m, slot, place):
        remote(
            res_send.at[b, m], res_recv.at[b, slot], s_send.at[b, m], s_recv.at[b, slot], place
        ).start()

    def give(b, m, value):
        res_send[b, m] = value.astype(BF16)

    def give_turned(b, m, value):
        res_send[b, m, pl.ds(0, CH), :] = value[:CH].T.astype(BF16)
        res_send[b, m, pl.ds(CH, CH), :] = (-value[CH:]).T.astype(BF16)

    half = lax.div(x, 2)

    def early(u):
        b, q = lax.div(u, PARTS), lax.rem(u, PARTS)
        turn(0, u, turned.at[u, 0])
        turn(1, u, turned.at[u, 1])
        add_product(2, 0, u, 1, (4,))
        add_product(0, 0, u, 0, (0, 1))
        add_product(1, 0, u, 0, (4,))

        @pl.when(q == PARTS - 1)
        def _():
            v = result(2, 0)
            give(b, 3, v)
            give_turned(b, 4, v)
            v = result(0, 1)
            give_turned(b, 0, v)
            keep(b, (1, 0), v)
            v = result(1, 0)
            give_turned(b, 1, v)
            keep(b, (0, 1), v)
            keep(b, (0, 0), result(0, 0))
            acc[0] = jnp.zeros_like(acc[0])
            for group in (1, 2):
                acc[group, :, pl.ds(0, CH)] = jnp.zeros((2 * CH, CH), F32)

    def send_early(b):
        for m, place in ((3, (1, 0)), (4, (0, 1)), (0, (1, 0)), (1, (0, 1))):
            send(b, m, m, place)

    def send_far(b):
        send(b, 5, 5, (2, 0))
        send(b, 6, 6, (0, 1))

    def send_both(b):
        send(b, 9, 9, (2, 0))
        send(b, 10, 9, (0, 2))

    def send_side(b):
        send(b, 7, 7, (0, 2))
        send(b, 8, 8, (1, 0))

    def send_diagonal(b):
        send(b, 2, 2, (1, 1))

    def late(u):
        b, q = lax.div(u, PARTS), lax.rem(u, PARTS)
        done = q == PARTS - 1
        now = done & (b == BINS - 1)
        turn(2, u, turned_far)

        @pl.when(b == half)
        def _():
            add_product(4, 0, u, 2, (4, 5))

        @pl.when(b != half)
        def _():
            add_product(4, 0, u, 2, (4,))

        @pl.when(done)
        def _():
            @pl.when(b == half)
            def _():
                v = result(4, 1)
                give(b, 9, v)
                give_turned(b, 10, v)
                pl.when(now)(lambda: send_both(b))

            v = result(4, 0)
            give(b, 5, v)
            give_turned(b, 6, v)
            pl.when(now)(lambda: send_far(b))

        add_product(2, 1, u, 1, (5,))

        @pl.when(done)
        def _():
            v = result(2, 1)
            give_turned(b, 7, v)
            give(b, 8, v)
            pl.when(now)(lambda: send_side(b))

        add_product(3, 0, u, 0, (2, 3))

        @pl.when(done)
        def _():
            v = result(3, 1)
            give_turned(b, 2, v)
            pl.when(now)(lambda: send_diagonal(b))
            keep(b, (1, 1), v)
            keep(b, (2, 0), result(3, 0))

        add_product(1, 1, u, 0, (5,))

        @pl.when(done)
        def _():
            keep(b, (0, 2), result(1, 1))
            for group in (1, 2):
                acc[group, :, pl.ds(CH, CH)] = jnp.zeros((2 * CH, CH), F32)
            for group in (3, 4):
                acc[group] = jnp.zeros_like(acc[group])

    def take(b):
        for slot in (3, 4, 0, 1, 9, 5, 6, 7, 8, 2):
            place = FOREIGN[slot]
            remote(
                res_recv.at[b, slot], res_recv.at[b, slot], s_send.at[b, slot], s_recv.at[b, slot], (0, 0)
            ).wait_recv()
            keep(b, place, res_recv[b, slot].astype(F32))

    loads[0].wait()
    loads[1].wait()
    whiten(0)
    pl.semaphore_wait(barrier, WIN - 1 + len(MATES))
    spread(0)
    acc[...] = jnp.zeros_like(acc)
    for q in range(1, PARTS):
        loads[1 + q].wait()
        whiten(q)
    for u in range(1, AHEAD):
        spread(u)

    def step(t, _):
        @pl.when(t < UNITS)
        def _():
            spread_all(t).wait_recv()
            for copy in direct(t):
                copy.start()

        @pl.when(t + AHEAD < UNITS)
        def _():
            spread(t + AHEAD)

        @pl.when((t >= 1) & (t <= UNITS))
        def _():
            here, onward = direct(t - 1), relay(t - 1)
            here[0].wait_recv()
            onward[0].start()
            onward[1].start()
            here[1].wait_recv()
            onward[2].start()
            onward[3].start()

        @pl.when((t >= EARLY) & (t < UNITS + EARLY))
        def _():
            early(t - EARLY)

        pl.when(t == UNITS)(lambda: send_early(1))
        pl.when(t == SEND_NEAR)(lambda: send_early(0))

        @pl.when(t == UNITS + 1)
        def _():
            for copy in relay(UNITS - 1):
                copy.wait_send()

        @pl.when(t == SEND_FAR)
        def _():
            send_far(0)
            send_side(0)
            send_diagonal(0)
            pl.when(half == 0)(lambda: send_both(0))

        @pl.when(t >= LATE)
        def _():
            for copy in relay(t - LATE):
                copy.wait_recv()
            late(t - LATE)

        return 0

    lax.fori_loop(0, UNITS + LATE, step, 0)
    take(0)

    def sent(u, _):
        spread_all(u).wait_send()
        for copy in direct(u):
            copy.wait_send()

        @pl.when(u < UNITS - 1)
        def _():
            for copy in relay(u):
                copy.wait_send()

        return 0

    lax.fori_loop(0, UNITS, sent, 0)

    def gone(b, m):
        remote(
            res_send.at[b, m], res_send.at[b, m], s_send.at[b, m], s_recv.at[b, 0], (0, 0)
        ).wait_send()

    for m in range(9):
        gone(0, m)
    pl.when(half == 0)(lambda: (gone(0, 9), gone(0, 10), None)[2])
    take(1)
    for m in range(9):
        gone(1, m)
    pl.when(half == 1)(lambda: (gone(1, 9), gone(1, 10), None)[2])


def body(spectra, quality_mask):
    flat = spectra.reshape(2, LW * FREQ, CH)
    dma = pltpu.SemaphoreType.DMA
    return pl.pallas_call(
        kernel,
        out_shape=pltpu.VMEM((BINS, 2, CH, CH * SIDE * SIDE), F32),
        in_specs=[pl.BlockSpec(memory_space=pltpu.HBM)] * 2,
        out_specs=pl.BlockSpec(memory_space=pltpu.VMEM),
        scratch_shapes=[
            pltpu.VMEM((2, LW * FREQ + FREQ, CH), F32),
            pltpu.VMEM((LW, CH), jnp.int32),
            pltpu.VMEM((UNITS, WIN, 2, PW, CH), BF16),
            pltpu.VMEM((len(PLACES), UNITS, 2, DEEP, CH), BF16),
            pltpu.VMEM((UNITS, 2, 2 * CH, 2 * DEEP), BF16),
            pltpu.VMEM((2 * CH, 2 * DEEP), BF16),
            pltpu.VMEM((5, 2 * CH, 2 * CH), F32),
            pltpu.VMEM((BINS, 11, 2 * CH, CH), BF16),
            pltpu.VMEM((BINS, 10, 2 * CH, CH), BF16),
            dma((PARTS + 1,)),
            dma((UNITS,)),
            dma((UNITS,)),
            dma((UNITS, 2)),
            dma((UNITS, 2)),
            dma((UNITS, 4)),
            dma((UNITS, 4)),
            dma((BINS, 11)),
            dma((BINS, 10)),
        ],
        compiler_params=pltpu.CompilerParams(
            collective_id=0, has_side_effects=True, vmem_limit_bytes=40 * 1024 * 1024
        ),
        cost_estimate=pl.CostEstimate(
            flops=5_200_000_000, bytes_accessed=6 * 1024 * 1024, transcendentals=0
        ),
    )(*(pltpu.with_memory_space_constraint(a, pltpu.HBM) for a in (flat, quality_mask)))


def solution(mesh):
    placed = (P(None, "win", None, "chan"), P("win", "chan"))
    return jax.shard_map(
        body, mesh=mesh, in_specs=placed, out_specs=P("win", None, "chan", None), check_vma=False
    )
```

```python
import jax
import jax.numpy as jnp
from jax import lax
from jax.experimental import pallas as pl
from jax.experimental.pallas import tpu as pltpu
from jax.sharding import PartitionSpec as P

MESH = pl.DeviceIdType.MESH
F32, BF16 = jnp.float32, jnp.bfloat16

WIN = 16
SIDE = 4
BINS = 2
FREQ = WIN * BINS
CH = 128
LW = 64
PARTS = 4
PW = LW // PARTS
AHEAD = 2
EARLY, LATE = 1, 3
SEND_NEAR, SEND_FAR = 9, 9
UNITS = BINS * PARTS
DEEP = WIN * PW
ROWS = PW * FREQ
SCALE = 1.0 / 32.0

PLACES = ((0, 0), (1, 0), (2, 0), (1, 1), (0, 1), (0, 2))
FOREIGN = ((-1, 0), (0, -1), (-1, -1), (-1, 1), (1, -1), (-2, 1), (2, -1), (1, -2), (-1, 2), (2, 2))
MATES = ((1, 0), (-1, 0), (2, 0), (0, 1), (0, -1), (0, 2), (1, 1), (-1, -1))


def kernel(
    spec, mask_hbm, out,
    spec_v, mask, send_v, g, turned, turned_far, acc, res_send, res_recv,
    in_sem, a_send, a_recv, d_send, d_recv, r_send, r_recv, s_send, s_recv,
):
    chan, win = lax.axis_index("chan"), lax.axis_index("win")
    x, y = lax.rem(chan, SIDE), lax.div(chan, SIDE)
    way = 1 - 2 * lax.rem(win, 2)

    def at(place):
        dx, dy = place
        return lax.rem(y + way * dy + 2 * SIDE, SIDE) * SIDE + lax.rem(x + way * dx + 2 * SIDE, SIDE)

    loads = [pltpu.make_async_copy(mask_hbm, mask, in_sem.at[PARTS])]
    for q in range(PARTS):
        rows = pl.ds(q * ROWS, ROWS)
        loads.append(pltpu.make_async_copy(spec.at[:, rows, :], spec_v.at[:, rows, :], in_sem.at[q]))
    for load in loads:
        load.start()

    barrier = pltpu.get_barrier_semaphore()

    def greet(k, _):
        pl.semaphore_signal(
            barrier, inc=1, device_id=(chan, lax.rem(win + k, WIN)), device_id_type=MESH
        )
        return 0

    lax.fori_loop(1, WIN, greet, 0)
    for place in MATES:
        pl.semaphore_signal(barrier, inc=1, device_id=(at(place), win), device_id_type=MESH)

    def level(q):
        def add(f, total):
            for p in range(2):
                v = spec_v[p, pl.ds(q * ROWS + f, PW, stride=FREQ), :]
                total = total + v * v
            return total

        total = lax.fori_loop(0, FREQ, add, jnp.zeros((PW, CH), F32), unroll=8)
        rms = jnp.sqrt(total * (1.0 / (2 * FREQ)) + 1e-6)
        return mask[pl.ds(q * PW, PW), :].astype(F32) / rms

    def whiten(q, factor, bins):
        def scale(dst, _):
            for b in bins:
                for p in range(2):
                    v = spec_v[p, pl.ds(q * ROWS + dst * BINS + b, PW, stride=FREQ), :]
                    send_v[b * PARTS + q, dst, p] = (v * factor).astype(BF16)
            return 0

        lax.fori_loop(0, WIN, scale, 0, unroll=4)

    mine = pl.ds(pl.multiple_of(win * PW, PW), PW)

    def spread(u):
        def one(k, _):
            apart = WIN // 2 + lax.div(k + 1, 2) * (1 - 2 * lax.rem(k, 2))
            dst = lax.rem(win + apart, WIN)
            pltpu.make_async_remote_copy(
                src_ref=send_v.at[u, dst], dst_ref=g.at[0, u, :, mine, :],
                send_sem=a_send.at[u], recv_sem=a_recv.at[u],
                device_id=(chan, dst), device_id_type=MESH,
            ).start()
            return 0

        lax.fori_loop(0, WIN - 1, one, 0)
        g[0, u, :, mine, :] = send_v[u, win]

    def spread_all(u):
        others = g.at[0, u, :, pl.ds(0, DEEP - PW), :]
        return pltpu.make_async_remote_copy(
            src_ref=others, dst_ref=others, send_sem=a_send.at[u], recv_sem=a_recv.at[u],
            device_id=(chan, win), device_id_type=MESH,
        )

    def remote(src, dst, send, recv, place):
        return pltpu.make_async_remote_copy(
            src_ref=src, dst_ref=dst, send_sem=send, recv_sem=recv,
            device_id=(at(place), win), device_id_type=MESH,
        )

    def direct(u):
        return [
            remote(g.at[0, u], g.at[slot, u], d_send.at[u, i], d_recv.at[u, i], place)
            for i, (slot, place) in enumerate(((1, (-1, 0)), (4, (0, -1))))
        ]

    def relay(u):
        moves = (
            (g.at[1, u], g.at[2, u], (-1, 0)),
            (g.at[1, u, 0], g.at[3, u, 0], (0, -1)),
            (g.at[4, u], g.at[5, u], (0, -1)),
            (g.at[4, u, 1], g.at[3, u, 1], (-1, 0)),
        )
        return [
            remote(src, dst, r_send.at[u, i], r_recv.at[u, i], place)
            for i, (src, dst, place) in enumerate(moves)
        ]

    def turn(slot, u, dst):
        a0, a1 = g[slot, u, 0].T, g[slot, u, 1].T
        dst[pl.ds(0, CH), pl.ds(0, DEEP)] = a0
        dst[pl.ds(0, CH), pl.ds(DEEP, DEEP)] = a1
        dst[pl.ds(CH, CH), pl.ds(0, DEEP)] = a1
        dst[pl.ds(CH, CH), pl.ds(DEEP, DEEP)] = -a0

    def add_product(group, at_col, u, lhs, right):
        rhs = [g[s, u].reshape(2 * DEEP, CH) for s in right]
        rhs = rhs[0] if len(rhs) == 1 else jnp.concatenate(rhs, axis=1)
        left = turned_far[...] if lhs == 2 else turned[u, lhs]
        part = jnp.dot(left, rhs, preferred_element_type=F32)
        acc[group, :, pl.ds(at_col * CH, CH * len(right))] += part

    def result(group, i):
        return acc[group, :, pl.ds(i * CH, CH)] * SCALE

    def column(place):
        return pl.ds(pl.multiple_of(at(place) * CH, CH), CH)

    def keep(b, place, value):
        for k in range(2):
            out[b, k, :, column(place)] = value[k * CH : (k + 1) * CH]

    def send(b, m, slot, place):
        remote(
            res_send.at[b, m], res_recv.at[b, slot], s_send.at[b, m], s_recv.at[b, slot], place
        ).start()

    def give(b, m, value):
        res_send[b, m] = value.astype(BF16)

    def give_turned(b, m, value):
        res_send[b, m, pl.ds(0, CH), :] = value[:CH].T.astype(BF16)
        res_send[b, m, pl.ds(CH, CH), :] = (-value[CH:]).T.astype(BF16)

    half = lax.div(x, 2)

    def early(u):
        b, q = lax.div(u, PARTS), lax.rem(u, PARTS)
        turn(0, u, turned.at[u, 0])
        turn(1, u, turned.at[u, 1])
        add_product(2, 0, u, 1, (4,))
        add_product(0, 0, u, 0, (0, 1))
        add_product(1, 0, u, 0, (4,))

        @pl.when(q == PARTS - 1)
        def _():
            v = result(2, 0)
            give(b, 3, v)
            give_turned(b, 4, v)
            v = result(0, 1)
            give_turned(b, 0, v)
            keep(b, (1, 0), v)
            v = result(1, 0)
            give_turned(b, 1, v)
            keep(b, (0, 1), v)
            keep(b, (0, 0), result(0, 0))
            acc[0] = jnp.zeros_like(acc[0])
            for group in (1, 2):
                acc[group, :, pl.ds(0, CH)] = jnp.zeros((2 * CH, CH), F32)

    def send_early(b):
        for m, place in ((3, (1, 0)), (4, (0, 1)), (0, (1, 0)), (1, (0, 1))):
            send(b, m, m, place)

    def send_far(b):
        send(b, 5, 5, (2, 0))
        send(b, 6, 6, (0, 1))

    def send_both(b):
        send(b, 9, 9, (2, 0))
        send(b, 10, 9, (0, 2))

    def send_side(b):
        send(b, 7, 7, (0, 2))
        send(b, 8, 8, (1, 0))

    def send_diagonal(b):
        send(b, 2, 2, (1, 1))

    def late(u):
        b, q = lax.div(u, PARTS), lax.rem(u, PARTS)
        done = q == PARTS - 1
        now = done & (b == BINS - 1)
        turn(2, u, turned_far)

        @pl.when(b == half)
        def _():
            add_product(4, 0, u, 2, (4, 5))

        @pl.when(b != half)
        def _():
            add_product(4, 0, u, 2, (4,))

        @pl.when(done)
        def _():
            @pl.when(b == half)
            def _():
                v = result(4, 1)
                give(b, 9, v)
                give_turned(b, 10, v)
                pl.when(now)(lambda: send_both(b))

            v = result(4, 0)
            give(b, 5, v)
            give_turned(b, 6, v)
            pl.when(now)(lambda: send_far(b))

        add_product(2, 1, u, 1, (5,))

        @pl.when(done)
        def _():
            v = result(2, 1)
            give_turned(b, 7, v)
            give(b, 8, v)
            pl.when(now)(lambda: send_side(b))

        add_product(3, 0, u, 0, (2, 3))

        @pl.when(done)
        def _():
            v = result(3, 1)
            give_turned(b, 2, v)
            pl.when(now)(lambda: send_diagonal(b))
            keep(b, (1, 1), v)
            keep(b, (2, 0), result(3, 0))

        add_product(1, 1, u, 0, (5,))

        @pl.when(done)
        def _():
            keep(b, (0, 2), result(1, 1))
            for group in (1, 2):
                acc[group, :, pl.ds(CH, CH)] = jnp.zeros((2 * CH, CH), F32)
            for group in (3, 4):
                acc[group] = jnp.zeros_like(acc[group])

    def take(b):
        for slot in (3, 4, 0, 1, 9, 5, 6, 7, 8, 2):
            place = FOREIGN[slot]
            remote(
                res_recv.at[b, slot], res_recv.at[b, slot], s_send.at[b, slot], s_recv.at[b, slot], (0, 0)
            ).wait_recv()
            keep(b, place, res_recv[b, slot].astype(F32))

    loads[0].wait()
    loads[1].wait()
    first = level(0)
    whiten(0, first, (0,))
    pl.semaphore_wait(barrier, WIN - 1 + len(MATES))
    spread(0)
    whiten(0, first, range(1, BINS))
    acc[...] = jnp.zeros_like(acc)
    for q in range(1, PARTS):
        loads[1 + q].wait()
        whiten(q, level(q), range(BINS))
    for u in range(1, AHEAD):
        spread(u)

    def step(t, _):
        @pl.when(t < UNITS)
        def _():
            spread_all(t).wait_recv()
            for copy in direct(t):
                copy.start()

        @pl.when(t + AHEAD < UNITS)
        def _():
            spread(t + AHEAD)

        @pl.when((t >= 1) & (t <= UNITS))
        def _():
            here, onward = direct(t - 1), relay(t - 1)
            here[0].wait_recv()
            onward[0].start()
            onward[1].start()
            here[1].wait_recv()
            onward[2].start()
            onward[3].start()

        @pl.when((t >= EARLY) & (t < UNITS + EARLY))
        def _():
            early(t - EARLY)

        pl.when(t == UNITS)(lambda: send_early(1))
        pl.when(t == SEND_NEAR)(lambda: send_early(0))

        @pl.when(t == UNITS + 1)
        def _():
            for copy in relay(UNITS - 1):
                copy.wait_send()

        @pl.when(t == SEND_FAR)
        def _():
            send_far(0)
            send_side(0)
            send_diagonal(0)
            pl.when(half == 0)(lambda: send_both(0))

        @pl.when(t >= LATE)
        def _():
            for copy in relay(t - LATE):
                copy.wait_recv()
            late(t - LATE)

        return 0

    lax.fori_loop(0, UNITS + LATE, step, 0)
    take(0)

    def sent(u, _):
        spread_all(u).wait_send()
        for copy in direct(u):
            copy.wait_send()

        @pl.when(u < UNITS - 1)
        def _():
            for copy in relay(u):
                copy.wait_send()

        return 0

    lax.fori_loop(0, UNITS, sent, 0)

    def gone(b, m):
        remote(
            res_send.at[b, m], res_send.at[b, m], s_send.at[b, m], s_recv.at[b, 0], (0, 0)
        ).wait_send()

    for m in range(9):
        gone(0, m)
    pl.when(half == 0)(lambda: (gone(0, 9), gone(0, 10), None)[2])
    take(1)
    for m in range(9):
        gone(1, m)
    pl.when(half == 1)(lambda: (gone(1, 9), gone(1, 10), None)[2])


def body(spectra, quality_mask):
    flat = spectra.reshape(2, LW * FREQ, CH)
    dma = pltpu.SemaphoreType.DMA
    return pl.pallas_call(
        kernel,
        out_shape=pltpu.VMEM((BINS, 2, CH, CH * SIDE * SIDE), F32),
        in_specs=[pl.BlockSpec(memory_space=pltpu.HBM)] * 2,
        out_specs=pl.BlockSpec(memory_space=pltpu.VMEM),
        scratch_shapes=[
            pltpu.VMEM((2, LW * FREQ + FREQ, CH), F32),
            pltpu.VMEM((LW, CH), jnp.int32),
            pltpu.VMEM((UNITS, WIN, 2, PW, CH), BF16),
            pltpu.VMEM((len(PLACES), UNITS, 2, DEEP, CH), BF16),
            pltpu.VMEM((UNITS, 2, 2 * CH, 2 * DEEP), BF16),
            pltpu.VMEM((2 * CH, 2 * DEEP), BF16),
            pltpu.VMEM((5, 2 * CH, 2 * CH), F32),
            pltpu.VMEM((BINS, 11, 2 * CH, CH), BF16),
            pltpu.VMEM((BINS, 10, 2 * CH, CH), BF16),
            dma((PARTS + 1,)),
            dma((UNITS,)),
            dma((UNITS,)),
            dma((UNITS, 2)),
            dma((UNITS, 2)),
            dma((UNITS, 4)),
            dma((UNITS, 4)),
            dma((BINS, 11)),
            dma((BINS, 10)),
        ],
        compiler_params=pltpu.CompilerParams(
            collective_id=0, has_side_effects=True, vmem_limit_bytes=40 * 1024 * 1024
        ),
        cost_estimate=pl.CostEstimate(
            flops=5_200_000_000, bytes_accessed=6 * 1024 * 1024, transcendentals=0
        ),
    )(*(pltpu.with_memory_space_constraint(a, pltpu.HBM) for a in (flat, quality_mask)))


def solution(mesh):
    placed = (P(None, "win", None, "chan"), P("win", "chan"))
    return jax.shard_map(
        body, mesh=mesh, in_specs=placed, out_specs=P("win", None, "chan", None), check_vma=False
    )
```
